128 devices in a mesh: leaf: 32 (over y, z, core), sub: 4 (over x).
Axes of the slice: x: 4, y: 4, z: 4, core: 2. Of those that a mesh axis runs over, the one named last changes fastest.
Arguments:
- points: float32 [3, 131072], P(None, ('leaf', 'sub')), may hold values from 0 to 4
- order: int32 [128, 1024], P(('leaf', 'sub')), may hold values from 0 to 1023, each once within a row
- counts: int32 [128], P(('leaf', 'sub')), may hold values from 1 to 1024, 98304 in all
- basis: float32 [131072, 896], P(('leaf', 'sub')), may hold values from -0.1875 to 0.1875
- right_side: float32 [131072, 128], P(('leaf', 'sub')), may hold values from -6 to 6
- coupling: float32 [7, 256, 256], replicated, may hold values from -0.375 to 0.375
Outputs:
- solution: float32 [131072, 128], P(('leaf', 'sub'))
The draws below stay inside these ranges and needn't reach their ends.
Inputs may be any that keep to these rules, and one draw needn't show every extreme that they name: `order`: each row orders the 1024 slots of one leaf, every slot once. `counts`: slots of a leaf at or past its count are padding; some leaf is full.
All inputs are finite; a program needn't handle non-finite values. No bound on the sum of `counts` on one device may be relied on, other than what follows from the above.
Results may differ from the reference program's by a relative error of at most 0.0003.
Values sent between devices are 32-bit elements; how exact they have to be, the bound alone decides.
A program may use at most 128 MiB of HBM per device.

```python
import math
import jax
import jax.numpy as jnp
import numpy as np
from jax import lax

R = 128
NRHS = 128
LEAF = 1024
LEAVES = 128
TOTAL = 131072
LEVELS = 7
COLS = 1024


def level_of(own_key, extent, pieces, low, largest):
    factor_of = 1.0
    for position, shards_of in pieces:
        draws = jax.random.uniform(jax.random.fold_in(jax.random.fold_in(own_key, 6), position), (shards_of,), jnp.float32, low / len(pieces), largest / len(pieces))
        factor_of = factor_of * jnp.repeat(jnp.exp(draws), extent[position] // shards_of).reshape((-1,) + (1,) * (len(extent) - 1 - position))
    return factor_of


def length_profile(count, total, most, skew):
    portions = [(1 << 20) // math.isqrt(grade ** skew) + 1 for grade in range(2, count + 1)]
    spare, given = total - most - (count - 1), [1] * (count - 1)
    while spare > 0:
        movable = [i for i in range(count - 1) if given[i] < most]
        mass, left = sum([portions[i] for i in movable]), spare
        for i in movable:
            extra = min(most - given[i], max(1, left * portions[i] // mass), spare)
            given[i] = given[i] + extra
            spare = spare - extra
    return np.array([most] + given)


def ragged(stream_key, number_of, total, most, slope):
    if number_of == 2:
        one = jax.random.randint(stream_key, (), max(1, total - most), min(most, total - 1) + 1)
        return jnp.stack([one, total - one])
    tallies = jnp.asarray(length_profile(number_of, total, most, slope), jnp.int32)
    twos = (number_of - 1) // 2
    source_of, taker = tallies[1:1 + 2 * twos:2], tallies[2:2 + 2 * twos:2]
    margin = jnp.minimum(source_of - 1, most - taker)
    moved = jax.random.randint(jax.random.fold_in(stream_key, 1), (twos,), 0, 1 << 20) % (margin + 1)
    tallies = tallies.at[1:1 + 2 * twos:2].set(source_of - moved).at[2:2 + 2 * twos:2].set(taker + moved)
    return tallies[jax.random.permutation(jax.random.fold_in(stream_key, 2), number_of)]


def centred(key, extent, spread, most, split=(), kind=jnp.bfloat16):
    result = jax.random.normal(key, extent, jnp.float32) * spread
    if len(split) > 0:
        result = level_of(key, extent, split, -0.22, 0.18) * result
    return jnp.clip(result, min=-most, max=most).astype(kind)


def setup_inputs(seed: int = 0) -> dict:
    seeds = jax.random.split(jax.random.key(seed), 7)
    points = jnp.clip(4.0 * jax.random.uniform(seeds[0], (3, TOTAL), jnp.float32) ** level_of(seeds[0], (3, TOTAL), ((1, 128),), -0.2, 0.2), 0.0, 4.0)
    order = jax.vmap(lambda own: jax.random.permutation(own, LEAF))(jax.random.split(seeds[1], LEAVES)).reshape((LEAVES, LEAF)).astype(jnp.int32)
    counts = ragged(seeds[2], LEAVES, 3 * LEAVES * LEAF // 4, LEAF, 1).astype(jnp.int32)
    basis = centred(seeds[3], (TOTAL, LEVELS * R), LEAF ** -0.5, 0.1875, ((0, 128),), jnp.float32)
    right_side = centred(seeds[4], (TOTAL, NRHS), 1.0, 6.0, ((0, 128),), jnp.float32)
    coupling = centred(seeds[5], (LEVELS, 2 * R, 2 * R), (2 * R) ** -0.5, 0.375, (), jnp.float32)
    return {"points": points, "order": order, "counts": counts, "basis": basis, "right_side": right_side, "coupling": coupling}


GAMMA_RATE = 2.0
NUGGET_VALUE = 1.0

def leaf_solve(packed):
    coords, ordering, count, basis_rows, rhs_rows = packed
    ordered = coords[:, ordering]
    live_mask = (jnp.arange(coords.shape[1]) < count).astype(jnp.float32)
    offsets = ordered[:, :, None] - ordered[:, None, :]
    distance = jnp.sum(offsets * offsets, axis=0)
    kernel = jnp.exp(-GAMMA_RATE * distance) * live_mask[:, None] * live_mask[None, :]
    kernel = kernel + NUGGET_VALUE * jnp.eye(coords.shape[1], dtype=jnp.float32)
    lower_tri = jnp.linalg.cholesky(kernel)
    stacked = jnp.concatenate([basis_rows, rhs_rows], axis=1) * live_mask[:, None]
    solved = jax.scipy.linalg.cho_solve((lower_tri, True), stacked)
    return (solved, stacked[:, :basis_rows.shape[1]])

def couple(first_sums, second_sums, factor):
    upper_half = factor[:R]
    lower_half = factor[R:]
    highest = lax.Precision.HIGHEST
    first_block = first_sums[:, :R]
    second_block = second_sums[:, :R]
    coupled = jnp.eye(2 * R, dtype=jnp.float32)
    coupled = coupled + jnp.dot(upper_half.T, jnp.dot(first_block, upper_half, precision=highest), precision=highest)
    coupled = coupled + jnp.dot(lower_half.T, jnp.dot(second_block, lower_half, precision=highest), precision=highest)
    coupled = 0.5 * (coupled + coupled.T)
    forcing = jnp.dot(upper_half.T, first_sums, precision=highest) + jnp.dot(lower_half.T, second_sums, precision=highest)
    lower_tri = jnp.linalg.cholesky(coupled)
    solved_coef = jax.scipy.linalg.cho_solve((lower_tri, True), forcing)
    return jnp.dot(factor, solved_coef, precision=highest)

def reference(points, order, counts, basis, right_side, coupling):
    highest = lax.Precision.HIGHEST
    coords = points.reshape(3, LEAVES, LEAF).transpose(1, 0, 2)
    solved, masked = lax.map(leaf_solve, (coords, order, counts, basis.reshape(LEAVES, LEAF, LEVELS * R), right_side.reshape(LEAVES, LEAF, NRHS)))
    for tree_level in range(LEVELS):
        col_start = tree_level * R
        span_cols = COLS - col_start
        group_size = 2 ** tree_level
        block_rows = masked[:, :, col_start:col_start + R]
        projected = jnp.einsum('gnr,gnc->grc', block_rows, solved[:, :, col_start:], precision=highest)
        child_sums = projected.reshape(LEAVES // group_size, group_size, R, span_cols).sum(axis=1)
        paired = child_sums.reshape(LEAVES // (2 * group_size), 2, R, span_cols)
        mixed = jax.vmap(couple, in_axes=(0, 0, None))(paired[:, 0], paired[:, 1], coupling[tree_level])
        per_child = mixed.reshape(LEAVES // group_size, R, span_cols)
        per_leaf = jnp.repeat(per_child, group_size, axis=0)
        basis_part = solved[:, :, col_start:col_start + R]
        update = jnp.einsum('gnr,grc->gnc', basis_part, per_leaf, precision=highest)
        solved = solved.at[:, :, col_start:].add(-update)
    return solved[:, :, LEVELS * R:].reshape(TOTAL, NRHS)
```

```python
import functools

import jax
import jax.numpy as jnp
from jax import lax
from jax.experimental import pallas as pl
from jax.experimental.pallas import tpu as pltpu
from jax.sharding import PartitionSpec as P

R = 128
GAMMA_RATE = 2.0
NUGGET_VALUE = 1.0
F32 = jnp.float32
BF16 = jnp.bfloat16
VMEM = pl.BlockSpec(memory_space=pltpu.VMEM)
SMEM = pl.BlockSpec(memory_space=pltpu.SMEM)
PARAMS = pltpu.CompilerParams(vmem_limit_bytes=56 * 1024 * 1024)


def split(x):
    high = x.astype(BF16)
    low = (x - high.astype(F32)).astype(BF16)
    return high, low


def dot(a, b):
    return jnp.dot(a, b, preferred_element_type=F32)


def wide(x):
    high, low = split(x)
    return jnp.concatenate([high, high, low], axis=1)


def tall(x):
    high, low = split(x)
    return jnp.concatenate([high, low, high], axis=0)


def dot3(a, b):
    return dot(wide(a), tall(b))


def identity(n):
    rows = lax.broadcasted_iota(jnp.int32, (n, n), 0)
    cols = lax.broadcasted_iota(jnp.int32, (n, n), 1)
    return (rows == cols).astype(F32)


def factor(a_ref, j_ref):
    n = R
    groups = n // 8
    j_ref[...] = identity(n)
    sub = lax.broadcasted_iota(jnp.int32, (8, n), 0)
    for p in range(groups):
        r0 = 8 * p
        panel = a_ref[r0 : r0 + 8, :]
        eye_p = j_ref[r0 : r0 + 8, :]
        cols = [jnp.broadcast_to(panel[:, r0 + c : r0 + c + 1], (8, n)) for c in range(8)]
        a = [[jnp.broadcast_to(cols[c][s : s + 1, :], (8, n)) for c in range(s + 1)] for s in range(8)]
        rs = [None] * 8
        low = [[None] * 8 for _ in range(8)]
        for r in range(8):
            rs[r] = lax.rsqrt(a[r][r])
            for s in range(r + 1, 8):
                low[s][r] = a[s][r] * rs[r]
            for s in range(r + 1, 8):
                for c in range(r + 1, s + 1):
                    a[s][c] = a[s][c] - low[s][r] * low[c][r]
        urow = []
        jrow = []
        for r in range(8):
            ur = jnp.broadcast_to(panel[r : r + 1, :], (8, n))
            jr = jnp.broadcast_to(eye_p[r : r + 1, :], (8, n))
            for k in range(r):
                ur = ur - low[r][k] * urow[k]
                jr = jr - low[r][k] * jrow[k]
            urow.append(ur * rs[r])
            jrow.append(jr * rs[r])
        done = jrow[0]
        for r in range(1, 8):
            done = jnp.where(sub == r, jrow[r], done)
        j_ref[r0 : r0 + 8, :] = done
        for g in range(p + 1, groups):
            ag = a_ref[8 * g : 8 * g + 8, :]
            jg = j_ref[8 * g : 8 * g + 8, :]
            acc_a, acc_j = ag, jg
            m = []
            for r in range(8):
                b = jnp.broadcast_to(ag[:, r0 + r : r0 + r + 1], (8, n))
                for k in range(r):
                    b = b - low[r][k] * m[k]
                m.append(b * rs[r])
                acc_a = acc_a - m[r] * urow[r]
                acc_j = acc_j - m[r] * jrow[r]
            a_ref[8 * g : 8 * g + 8, :] = acc_a
            j_ref[8 * g : 8 * g + 8, :] = acc_j


def chunks(start, stop, size=256):
    return [(c, min(c + size, stop)) for c in range(start, stop, size)]


def blk(i):
    return slice(i * R, (i + 1) * R)


def leaf_kernel(
    count_ref, xr_ref, xc_ref, basis_ref, rhs_ref,
    row_ref, trail_ref, y_ref, u_ref, li_ref,
    a_ref, j_ref, right_ref, left_ref, yh_ref, yl_ref,
):
    slots, columns = y_ref.shape
    nb = slots // R
    levels = basis_ref.shape[1] // R
    count = count_ref[0]
    live_lane = (lax.broadcasted_iota(jnp.int32, (1, slots), 1) < count).astype(F32)
    live_sub = (lax.broadcasted_iota(jnp.int32, (slots, 1), 0) < count).astype(F32)
    for b in range(nb):
        live_b = live_sub[blk(b), :]
        y_ref[blk(b), : levels * R] = basis_ref[blk(b), :] * live_b
        y_ref[blk(b), levels * R :] = rhs_ref[blk(b), :] * live_b
        for c0, c1 in chunks(b * R, slots, 128):
            dist = None
            for d in range(3):
                diff = xc_ref[blk(b), d : d + 1] - xr_ref[d : d + 1, c0:c1]
                dist = diff * diff if dist is None else dist + diff * diff
            kern = jnp.exp(-GAMMA_RATE * dist) * live_b * live_lane[:, c0:c1]
            if c0 == b * R:
                kern = kern + NUGGET_VALUE * identity(R)
            u_ref[blk(b), c0:c1] = kern

    def step(b, carry):
        here = pl.ds(pl.multiple_of(b * R, R), R)
        a_ref[...] = u_ref[here, here]
        factor(a_ref, j_ref)
        li_ref[here, :] = j_ref[...]
        for static_b in range(nb):

            @pl.when(b == static_b)
            def _(b=static_b):
                inv = wide(j_ref[...])
                for c0, c1 in chunks((b + 1) * R, slots, 256):
                    new = dot(inv, tall(u_ref[blk(b), c0:c1]))
                    u_ref[blk(b), c0:c1] = new
                    right_ref[:, c0:c1] = tall(new)
                    for e0, e1 in chunks(c0, c1, R):
                        left_ref[e0:e1, :] = wide(new[:, e0 - c0 : e1 - c0].T)
                for c0, c1 in chunks(0, columns, 256):
                    new = dot(inv, tall(y_ref[blk(b), c0:c1]))
                    y_ref[blk(b), c0:c1] = new
                    stacked = tall(new)
                    right_ref[:, slots + c0 : slots + c1] = stacked
                    yh_ref[blk(b), c0:c1] = stacked[:R]
                    yl_ref[blk(b), c0:c1] = stacked[R : 2 * R]
                for i in range(b + 1, nb):
                    left = left_ref[blk(i), :]
                    for c0, c1 in chunks(i * R, slots, 256):
                        u_ref[blk(i), c0:c1] = u_ref[blk(i), c0:c1] - dot(left, right_ref[:, c0:c1])
                    for c0, c1 in chunks(0, columns, 256):
                        y_ref[blk(i), c0:c1] = y_ref[blk(i), c0:c1] - dot(
                            left, right_ref[:, slots + c0 : slots + c1]
                        )

        return carry

    lax.fori_loop(0, nb, step, 0)
    offset = 0
    for k in range(levels):
        high, low = split(y_ref[:, blk(k)].T)
        target = row_ref if k == 0 else trail_ref
        base = 0 if k == 0 else offset
        for c0, c1 in chunks(k * R, columns, 256):
            yh = yh_ref[:, c0:c1]
            value = dot(high, yh) + dot(high, yl_ref[:, c0:c1]) + dot(low, yh)
            target[:, base + c0 - k * R : base + c1 - k * R] = value
        if k > 0:
            offset += columns - k * R


def level_kernel(own_ref, sib_ref, e_ref, side_ref, z_ref, w_ref, q_ref, a_ref, j_ref):
    width = own_ref.shape[1]
    side = side_ref[0]
    mine = pl.ds(pl.multiple_of(side * R, R), R)
    other = pl.ds(pl.multiple_of((1 - side) * R, R), R)
    q_ref[mine, :] = own_ref[...]
    q_ref[other, :] = sib_ref[...]
    e_stack = tall(e_ref[...])
    up = e_ref[:R, :].T
    low = e_ref[R:, :].T
    first = dot3(up, q_ref[:R, :R])
    second = dot3(low, q_ref[R:, :R])
    h = dot(wide(jnp.concatenate([first, second], axis=1)), e_stack)
    both = wide(jnp.concatenate([up, low], axis=1))
    forcing = dot(both, tall(q_ref[:, R:]))
    h12 = 0.5 * (h[:R, R:] + h[R:, :R].T)
    h11 = h[:R, :R]
    h22 = h[R:, R:]
    a_ref[...] = 0.5 * (h11 + h11.T) + identity(R)
    factor(a_ref, j_ref)
    inv1 = j_ref[...]
    inv1w = wide(inv1)
    u12 = dot(inv1w, tall(h12))
    u12t = u12.T
    a_ref[...] = 0.5 * (h22 + h22.T) + identity(R) - dot3(u12t, u12)
    z1 = dot(inv1w, tall(forcing[:R]))
    z_ref[:R, :] = z1
    rest = forcing[R:] - dot3(u12t, z1)
    factor(a_ref, j_ref)
    inv2 = j_ref[...]
    z_ref[R:, :] = dot3(inv2, rest)
    e_own = e_ref[mine, :]
    w1 = dot3(e_own[:, :R], inv1.T)
    w2 = dot3(e_own[:, R:] - dot3(w1, u12), inv2.T)
    w_ref[:, :R] = w1
    w_ref[:, R:] = w2


def next_row_kernel(own_ref, sib_ref, z_ref, row_ref):
    width = row_ref.shape[1]
    row_ref[...] = own_ref[:, :width] + sib_ref[:, :width] - dot3(z_ref[:, :R].T, z_ref[...])


def rest_kernel(own_ref, sib_ref, z_ref, w_ref, trail_ref, g_ref):
    width = z_ref.shape[1]
    source, target = width, 0
    for k in range(1, width // R - 1):
        size = width - k * R
        trail_ref[:, target : target + size] = (
            own_ref[:, source : source + size]
            + sib_ref[:, source : source + size]
            - dot3(z_ref[:, blk(k)].T, z_ref[:, k * R :])
        )
        source += size
        target += size
    g_ref[...] = dot3(w_ref[...], z_ref[...])


def g_kernel(z_ref, w_ref, g_ref):
    g_ref[...] = dot3(w_ref[...], z_ref[...])


def final_kernel(*refs):
    y_ref, u_ref, li_ref = refs[:3]
    levels = len(refs) - 6
    g_refs = refs[3 : 3 + levels]
    out_ref, v_ref, x_ref = refs[3 + levels :]
    slots = y_ref.shape[0]
    nb = slots // R
    for k in reversed(range(levels)):
        g = g_refs[k]
        value = -g[:, g.shape[1] - R :]
        if k < levels - 1:
            value = value - dot3(g[:, : g.shape[1] - R], v_ref[(k + 1) * R :, :])
        v_ref[blk(k), :] = value
    vt = tall(v_ref[...])
    for b in range(nb):
        x_ref[blk(b), :] = y_ref[blk(b), levels * R :] + dot(wide(y_ref[blk(b), : levels * R]), vt)
    for b in reversed(range(nb)):
        value = dot3(li_ref[blk(b), :].T, x_ref[blk(b), :])
        out_ref[blk(b), :] = value
        if b > 0:
            x_ref[: b * R, :] = x_ref[: b * R, :] - dot3(u_ref[: b * R, blk(b)], value)


def f32(*shape):
    return jax.ShapeDtypeStruct(shape, F32)


def call(kernel, outs, ins, scratch=(), **kw):
    return pl.pallas_call(
        kernel,
        out_shape=outs,
        in_specs=ins,
        out_specs=jax.tree.map(lambda _: VMEM, outs),
        scratch_shapes=list(scratch),
        compiler_params=PARAMS,
        **kw,
    )


def shards(points, order, counts, basis, right_side, coupling):
    slots = points.shape[1]
    levels = basis.shape[1] // R
    columns = levels * R + right_side.shape[1]
    ordered = points[:, order[0]]
    trail_width = sum(columns - k * R for k in range(1, levels))
    row, trail, y, u, li = call(
        leaf_kernel,
        (f32(R, columns), f32(R, trail_width), f32(slots, columns), f32(slots, slots), f32(slots, R)),
        [SMEM, VMEM, VMEM, VMEM, VMEM],
        [
            pltpu.VMEM((R, R), F32),
            pltpu.VMEM((R, R), F32),
            pltpu.VMEM((3 * R, slots + columns), BF16),
            pltpu.VMEM((slots, 3 * R), BF16),
            pltpu.VMEM((slots, columns), BF16),
            pltpu.VMEM((slots, columns), BF16),
        ],
    )(counts, ordered, ordered.T, basis, right_side)
    subs = lax.axis_size("sub")
    sub_bits = subs.bit_length() - 1
    position = lax.axis_index("leaf") * subs + lax.axis_index("sub")
    neighbour = {0: ("sub", 1), 1: ("sub", 3), 2: ("leaf", 1), 3: ("leaf", 2), 4: ("leaf", 6), 5: ("leaf", 8), 6: ("leaf", 24)}

    def swap(x, level):
        axis, mask = neighbour[level]
        return lax.ppermute(x, axis, [(i, i ^ mask) for i in range(lax.axis_size(axis))])

    gs = []
    for level in range(levels):
        last = level == levels - 1
        width = columns - (level + 1) * R
        sib = swap(row, level)
        if not last:
            sib_trail = swap(trail, level)
        side = (position >> level & 1).reshape(1)
        z, w = call(
            level_kernel,
            (f32(2 * R, width), f32(R, 2 * R)),
            [VMEM, VMEM, VMEM, SMEM],
            [pltpu.VMEM((2 * R, width + R), F32), pltpu.VMEM((R, R), F32), pltpu.VMEM((R, R), F32)],
            cost_estimate=pl.CostEstimate(flops=20_000_000_000, bytes_accessed=4_000_000, transcendentals=0),
        )(row, sib, coupling[level], side)
        if last:
            gs.append(call(g_kernel, f32(R, width), [VMEM, VMEM])(z, w))
        else:
            row = call(next_row_kernel, f32(R, width), [VMEM] * 3)(trail, sib_trail, z)
            if level < levels - 2:
                trail, g = call(rest_kernel, (f32(R, trail.shape[1] - width), f32(R, width)), [VMEM] * 4)(
                    trail, sib_trail, z, w
                )
            else:
                g = call(g_kernel, f32(R, width), [VMEM, VMEM])(z, w)
            gs.append(g)
    return call(
        final_kernel,
        f32(slots, columns - levels * R),
        [VMEM] * (3 + levels),
        [pltpu.VMEM((levels * R, R), F32), pltpu.VMEM((slots, R), F32)],
    )(y, u, li, *gs)


def solution(mesh):
    placed = (
        P(None, ("leaf", "sub")),
        P(("leaf", "sub"), None),
        P(("leaf", "sub")),
        P(("leaf", "sub"), None),
        P(("leaf", "sub"), None),
        P(),
    )
    return jax.shard_map(
        shards, mesh=mesh, in_specs=placed, out_specs=P(("leaf", "sub"), None), check_vma=False
    )
```

```python
import functools

import jax
import jax.numpy as jnp
from jax import lax
from jax.experimental import pallas as pl
from jax.experimental.pallas import tpu as pltpu
from jax.sharding import PartitionSpec as P

R = 128
GAMMA_RATE = 2.0
NUGGET_VALUE = 1.0
F32 = jnp.float32
BF16 = jnp.bfloat16
VMEM = pl.BlockSpec(memory_space=pltpu.VMEM)
SMEM = pl.BlockSpec(memory_space=pltpu.SMEM)
PARAMS = pltpu.CompilerParams(vmem_limit_bytes=56 * 1024 * 1024)


def split(x):
    high = x.astype(BF16)
    low = (x - high.astype(F32)).astype(BF16)
    return high, low


def dot(a, b):
    return jnp.dot(a, b, preferred_element_type=F32)


def wide(x):
    high, low = split(x)
    return jnp.concatenate([high, high, low], axis=1)


def tall(x):
    high, low = split(x)
    return jnp.concatenate([high, low, high], axis=0)


def dot3(a, b):
    return dot(wide(a), tall(b))


def identity(n):
    rows = lax.broadcasted_iota(jnp.int32, (n, n), 0)
    cols = lax.broadcasted_iota(jnp.int32, (n, n), 1)
    return (rows == cols).astype(F32)


def factor(a_ref, j_ref):
    n = R
    groups = n // 8
    j_ref[...] = identity(n)
    sub = lax.broadcasted_iota(jnp.int32, (8, n), 0)
    for p in range(groups):
        r0 = 8 * p
        panel = a_ref[r0 : r0 + 8, :]
        eye_p = j_ref[r0 : r0 + 8, :]
        cols = [jnp.broadcast_to(panel[:, r0 + c : r0 + c + 1], (8, n)) for c in range(8)]
        a = [[jnp.broadcast_to(cols[c][s : s + 1, :], (8, n)) for c in range(s + 1)] for s in range(8)]
        rs = [None] * 8
        low = [[None] * 8 for _ in range(8)]
        for r in range(8):
            rs[r] = lax.rsqrt(a[r][r])
            for s in range(r + 1, 8):
                low[s][r] = a[s][r] * rs[r]
            for s in range(r + 1, 8):
                for c in range(r + 1, s + 1):
                    a[s][c] = a[s][c] - low[s][r] * low[c][r]
        urow = []
        jrow = []
        for r in range(8):
            ur = jnp.broadcast_to(panel[r : r + 1, :], (8, n))
            jr = jnp.broadcast_to(eye_p[r : r + 1, :], (8, n))
            for k in range(r):
                ur = ur - low[r][k] * urow[k]
                jr = jr - low[r][k] * jrow[k]
            urow.append(ur * rs[r])
            jrow.append(jr * rs[r])
        done = jrow[0]
        for r in range(1, 8):
            done = jnp.where(sub == r, jrow[r], done)
        j_ref[r0 : r0 + 8, :] = done
        for g in range(p + 1, groups):
            ag = a_ref[8 * g : 8 * g + 8, :]
            jg = j_ref[8 * g : 8 * g + 8, :]
            acc_a, acc_j = ag, jg
            m = []
            for r in range(8):
                b = jnp.broadcast_to(ag[:, r0 + r : r0 + r + 1], (8, n))
                for k in range(r):
                    b = b - low[r][k] * m[k]
                m.append(b * rs[r])
                acc_a = acc_a - m[r] * urow[r]
                acc_j = acc_j - m[r] * jrow[r]
            a_ref[8 * g : 8 * g + 8, :] = acc_a
            j_ref[8 * g : 8 * g + 8, :] = acc_j


def chunks(start, stop, size=256):
    return [(c, min(c + size, stop)) for c in range(start, stop, size)]


def blk(i):
    return slice(i * R, (i + 1) * R)


def leaf_kernel(
    count_ref, xr_ref, xc_ref, basis_ref, rhs_ref,
    t_ref, y_ref, u_ref, li_ref,
    a_ref, j_ref, right_ref, left_ref, yh_ref, yl_ref,
):
    slots, columns = y_ref.shape
    nb = slots // R
    levels = basis_ref.shape[1] // R
    count = count_ref[0]
    live_lane = (lax.broadcasted_iota(jnp.int32, (1, slots), 1) < count).astype(F32)
    live_sub = (lax.broadcasted_iota(jnp.int32, (slots, 1), 0) < count).astype(F32)
    for b in range(nb):
        live_b = live_sub[blk(b), :]
        y_ref[blk(b), : levels * R] = basis_ref[blk(b), :] * live_b
        y_ref[blk(b), levels * R :] = rhs_ref[blk(b), :] * live_b
        for c0, c1 in chunks(b * R, slots, 128):
            dist = None
            for d in range(3):
                diff = xc_ref[blk(b), d : d + 1] - xr_ref[d : d + 1, c0:c1]
                dist = diff * diff if dist is None else dist + diff * diff
            kern = jnp.exp(-GAMMA_RATE * dist) * live_b * live_lane[:, c0:c1]
            if c0 == b * R:
                kern = kern + NUGGET_VALUE * identity(R)
            u_ref[blk(b), c0:c1] = kern

    def step(b, carry):
        here = pl.ds(pl.multiple_of(b * R, R), R)
        a_ref[...] = u_ref[here, here]
        factor(a_ref, j_ref)
        li_ref[here, :] = j_ref[...]
        for static_b in range(nb):

            @pl.when(b == static_b)
            def _(b=static_b):
                inv = wide(j_ref[...])
                for c0, c1 in chunks((b + 1) * R, slots, 256):
                    new = dot(inv, tall(u_ref[blk(b), c0:c1]))
                    u_ref[blk(b), c0:c1] = new
                    right_ref[:, c0:c1] = tall(new)
                    for e0, e1 in chunks(c0, c1, R):
                        left_ref[e0:e1, :] = wide(new[:, e0 - c0 : e1 - c0].T)
                for c0, c1 in chunks(0, columns, 256):
                    new = dot(inv, tall(y_ref[blk(b), c0:c1]))
                    y_ref[blk(b), c0:c1] = new
                    stacked = tall(new)
                    right_ref[:, slots + c0 : slots + c1] = stacked
                    yh_ref[blk(b), c0:c1] = stacked[:R]
                    yl_ref[blk(b), c0:c1] = stacked[R : 2 * R]
                for i in range(b + 1, nb):
                    left = left_ref[blk(i), :]
                    for c0, c1 in chunks(i * R, slots, 256):
                        u_ref[blk(i), c0:c1] = u_ref[blk(i), c0:c1] - dot(left, right_ref[:, c0:c1])
                    for c0, c1 in chunks(0, columns, 256):
                        y_ref[blk(i), c0:c1] = y_ref[blk(i), c0:c1] - dot(
                            left, right_ref[:, slots + c0 : slots + c1]
                        )

        return carry

    lax.fori_loop(0, nb, step, 0)
    offset = 0
    for k in range(levels):
        high, low = split(y_ref[:, blk(k)].T)
        for c0, c1 in chunks(k * R, columns, 256):
            yh = yh_ref[:, c0:c1]
            value = dot(high, yh) + dot(high, yl_ref[:, c0:c1]) + dot(low, yh)
            t_ref[:, offset + c0 - k * R : offset + c1 - k * R] = value
        offset += columns - k * R


def width_of(level, row, levels):
    return sum((levels + 1 - k) * R for k in range(level, row))


def levels_kernel(
    levels, t_ref, e_ref, g_ref,
    own_ref, sib_ref, zt_ref, zl_ref, bd_ref, h_ref, f_ref, eb_ref, et_ref, u_ref, inv_ref, a_ref, j_ref,
    send_sem, recv_sem,
):
    leaf, sub = lax.axis_index("leaf"), lax.axis_index("sub")
    core, z, y = leaf % 2, (leaf // 2) % 4, leaf // 8
    partner = [
        (leaf, sub + 1 - 2 * (sub % 2)),
        (leaf, 3 - sub),
        (leaf + 1 - 2 * core, sub),
        (y * 8 + (z + 1 - 2 * (z % 2)) * 2 + core, sub),
        (y * 8 + (3 - z) * 2 + core, sub),
        ((y + 1 - 2 * (y % 2)) * 8 + z * 2 + core, sub),
        ((3 - y) * 8 + z * 2 + core, sub),
    ]
    position = leaf * 4 + sub
    total = [width_of(k, levels, levels) for k in range(levels)]
    own_base = [0] + [sum(total[1:k]) for k in range(1, levels)]
    sib_base = [sum(total[:k]) for k in range(levels)]
    z_base = [sum((levels - j) * R for j in range(k)) for k in range(levels)]
    first_message = [sum(levels + 1 - j for j in range(k)) for k in range(levels)]

    def span(level, part):
        if part == 0:
            return 0, R
        start = R if part == 1 else width_of(level, level + part - 1, levels)
        return start, width_of(level, level + part, levels) if part > 1 else width_of(level, level + 1, levels)

    def own(level, c0, c1):
        ref = t_ref if level == 0 else own_ref
        return ref.at[:, own_base[level] + c0 : own_base[level] + c1]

    def sib(level, c0, c1):
        return sib_ref.at[:, sib_base[level] + c0 : sib_base[level] + c1]

    def message(level, part):
        c0, c1 = span(level, part)
        index = first_message[level] + part
        return pltpu.make_async_remote_copy(
            src_ref=own(level, c0, c1),
            dst_ref=sib(level, c0, c1),
            send_sem=send_sem.at[index],
            recv_sem=recv_sem.at[index],
            device_id=partner[level],
            device_id_type=pl.DeviceIdType.MESH,
        )

    def side_slices(level):
        side = (position // 2**level) % 2
        mine = pl.ds(pl.multiple_of(side * R, R), R)
        other = pl.ds(pl.multiple_of((1 - side) * R, R), R)
        return mine, other

    def prepare(level):
        e = e_ref[level]
        eb_ref[...] = wide(jnp.concatenate([e[:R].T, e[R:].T], axis=1))
        et_ref[...] = tall(e)

    def begin(level):
        mine, other = side_slices(level)
        bd_ref[mine, other] = jnp.zeros((R, R), F32)
        bd_ref[other, mine] = jnp.zeros((R, R), F32)
        bd_ref[mine, mine] = own(level, 0, R)[...]
        message(level, 0).wait_recv()
        bd_ref[other, other] = sib(level, 0, R)[...]
        x = dot(eb_ref[...], tall(bd_ref[...]))
        h = dot(wide(x), et_ref[...])
        h = 0.5 * (h + h.T)
        a_ref[...] = h[:R, :R] + identity(R)
        h_ref[:R, :] = h[:R, R:]
        h_ref[R:, :] = h[R:, R:]

    def half(level):
        mine, other = side_slices(level)
        inverse = j_ref[...]
        inv_ref[...] = inverse
        stacked = wide(inverse)
        upper = dot(stacked, tall(h_ref[:R, :]))
        ut = upper.T
        u_ref[...] = upper
        left = wide(ut)
        a_ref[...] = h_ref[R:, :] + identity(R) - dot(left, tall(upper))
        message(level, 1).wait_recv()
        w = (levels - level) * R
        f_ref[mine, :w] = own(level, R, R + w)[...]
        f_ref[other, :w] = sib(level, R, R + w)[...]
        zb = z_base[level]
        for c0, c1 in chunks(0, w):
            forcing = dot(eb_ref[...], tall(f_ref[:, c0:c1]))
            z1 = dot(stacked, tall(forcing[:R]))
            f_ref[:R, c0:c1] = z1
            f_ref[R:, c0:c1] = forcing[R:] - dot(left, tall(z1))

    def finish(level):
        w = (levels - level) * R
        zb = z_base[level]
        stacked = wide(j_ref[...])
        for c0, c1 in chunks(0, w):
            f_ref[R:, c0:c1] = dot(stacked, tall(f_ref[R:, c0:c1]))
            value = f_ref[:, c0:c1]
            zt_ref[:, zb + c0 : zb + c1] = tall(value)
            zl_ref[zb + c0 : zb + c1, :] = wide(value.T)

    def update(level, row):
        part = row - level + 1
        message(level, part).wait_recv()
        c0, c1 = span(level, part)
        n0 = width_of(level + 1, row, levels)
        zb = z_base[level]
        shift = (row - level - 1) * R
        left = zl_ref[zb + shift : zb + shift + R, :]
        for d0, d1 in chunks(0, c1 - c0):
            value = own(level, c0 + d0, c0 + d1)[...] + sib(level, c0 + d0, c0 + d1)[...]
            value = value - dot(left, zt_ref[:, zb + shift + d0 : zb + shift + d1])
            own(level + 1, n0 + d0, n0 + d1)[...] = value
        if row == level + 1:
            message(level + 1, 0).start()
            message(level + 1, 1).start()
        else:
            message(level + 1, row - level).start()

    def gains(level):
        mine, _ = side_slices(level)
        e_own = e_ref[level, mine, :]
        w1 = dot3(e_own[:, :R], inv_ref[...].T)
        w2 = dot3(e_own[:, R:] - dot3(w1, u_ref[...]), j_ref[...].T)
        w = wide(jnp.concatenate([w1, w2], axis=1))
        zb = z_base[level]
        for c0, c1 in chunks(0, (levels - level) * R):
            g_ref[:, zb + c0 : zb + c1] = dot(w, zt_ref[:, zb + c0 : zb + c1])

    barrier = pltpu.get_barrier_semaphore()
    for device in partner:
        pl.semaphore_signal(barrier, inc=1, device_id=device, device_id_type=pl.DeviceIdType.MESH)
    pl.semaphore_wait(barrier, levels)
    for part in range(levels + 1):
        message(0, part).start()
    prepare(0)
    begin(0)

    late = {
        (1, 0): [(0, 2)],
        (1, 1): [(0, 3)],
        (2, 0): [(0, 4), (0, 5)],
        (2, 1): [(0, 6), (1, 3)],
        (3, 0): [(1, 4), (1, 5), (1, 6), (2, 4)],
        (4, 0): [(2, 5), (2, 6), (3, 5), (3, 6)],
        (5, 0): [(4, 6)],
    }

    def step(i, carry):
        factor(a_ref, j_ref)
        for level in range(levels):

            @pl.when(i == 2 * level)
            def _(level=level):
                half(level)
                for pair in late.get((level, 0), []):
                    update(*pair)

            @pl.when(i == 2 * level + 1)
            def _(level=level):
                finish(level)
                for pair in late.get((level, 1), []):
                    update(*pair)
                if level < levels - 1:
                    update(level, level + 1)
                    prepare(level + 1)
                gains(level)
                if level < levels - 1:
                    begin(level + 1)

        return carry

    lax.fori_loop(0, 2 * levels, step, 0)
    for level in range(levels):
        for part in range(levels + 1 - level):
            message(level, part).wait_send()


def final_kernel(y_ref, u_ref, li_ref, g_ref, out_ref, v_ref, x_ref):
    levels = y_ref.shape[1] // R - 1
    slots = y_ref.shape[0]
    nb = slots // R
    for k in reversed(range(levels)):
        base = sum((levels - j) * R for j in range(k))
        inner = (levels - 1 - k) * R
        value = -g_ref[:, base + inner : base + inner + R]
        if inner > 0:
            value = value - dot3(g_ref[:, base : base + inner], v_ref[(k + 1) * R :, :])
        v_ref[blk(k), :] = value
    vt = tall(v_ref[...])
    for b in range(nb):
        x_ref[blk(b), :] = y_ref[blk(b), levels * R :] + dot(wide(y_ref[blk(b), : levels * R]), vt)
    for b in reversed(range(nb)):
        value = dot3(li_ref[blk(b), :].T, x_ref[blk(b), :])
        out_ref[blk(b), :] = value
        if b > 0:
            x_ref[: b * R, :] = x_ref[: b * R, :] - dot3(u_ref[: b * R, blk(b)], value)


def f32(*shape):
    return jax.ShapeDtypeStruct(shape, F32)


def call(kernel, outs, ins, scratch=(), params=PARAMS, **kw):
    return pl.pallas_call(
        kernel,
        out_shape=outs,
        in_specs=ins,
        out_specs=jax.tree.map(lambda _: VMEM, outs),
        scratch_shapes=list(scratch),
        compiler_params=params,
        **kw,
    )


def shards(points, order, counts, basis, right_side, coupling):
    slots = points.shape[1]
    levels = basis.shape[1] // R
    columns = levels * R + right_side.shape[1]
    ordered = points[:, order[0]]
    packed = width_of(0, levels, levels)
    t, y, u, li = call(
        leaf_kernel,
        (f32(R, packed), f32(slots, columns), f32(slots, slots), f32(slots, R)),
        [SMEM, VMEM, VMEM, VMEM, VMEM],
        [
            pltpu.VMEM((R, R), F32),
            pltpu.VMEM((R, R), F32),
            pltpu.VMEM((3 * R, slots + columns), BF16),
            pltpu.VMEM((slots, 3 * R), BF16),
            pltpu.VMEM((slots, columns), BF16),
            pltpu.VMEM((slots, columns), BF16),
        ],
    )(counts, ordered, ordered.T, basis, right_side)
    own_width = sum(width_of(k, levels, levels) for k in range(1, levels))
    gain_width = sum((levels - k) * R for k in range(levels))
    messages = sum(levels + 1 - k for k in range(levels))
    g = call(
        functools.partial(levels_kernel, levels),
        f32(R, gain_width),
        [VMEM, VMEM],
        [
            pltpu.VMEM((R, own_width), F32),
            pltpu.VMEM((R, own_width + packed), F32),
            pltpu.VMEM((6 * R, gain_width), BF16),
            pltpu.VMEM((gain_width, 6 * R), BF16),
            pltpu.VMEM((2 * R, 2 * R), F32),
            pltpu.VMEM((2 * R, R), F32),
            pltpu.VMEM((2 * R, levels * R), F32),
            pltpu.VMEM((2 * R, 6 * R), BF16),
            pltpu.VMEM((6 * R, 2 * R), BF16),
            pltpu.VMEM((R, R), F32),
            pltpu.VMEM((R, R), F32),
            pltpu.VMEM((R, R), F32),
            pltpu.VMEM((R, R), F32),
            pltpu.SemaphoreType.DMA((messages,)),
            pltpu.SemaphoreType.DMA((messages,)),
        ],
        pltpu.CompilerParams(
            vmem_limit_bytes=56 * 1024 * 1024, collective_id=0, has_side_effects=True
        ),
    )(t, coupling)
    return call(
        final_kernel,
        f32(slots, columns - levels * R),
        [VMEM] * 4,
        [pltpu.VMEM((levels * R, R), F32), pltpu.VMEM((slots, R), F32)],
    )(y, u, li, g)


def solution(mesh):
    placed = (
        P(None, ("leaf", "sub")),
        P(("leaf", "sub"), None),
        P(("leaf", "sub")),
        P(("leaf", "sub"), None),
        P(("leaf", "sub"), None),
        P(),
    )
    return jax.shard_map(
        shards, mesh=mesh, in_specs=placed, out_specs=P(("leaf", "sub"), None), check_vma=False
    )
```

```python
import functools

import jax
import jax.numpy as jnp
from jax import lax
from jax.experimental import pallas as pl
from jax.experimental.pallas import tpu as pltpu
from jax.sharding import PartitionSpec as P

R = 128
GAMMA_RATE = 2.0
NUGGET_VALUE = 1.0
F32 = jnp.float32
BF16 = jnp.bfloat16
VMEM = pl.BlockSpec(memory_space=pltpu.VMEM)
SMEM = pl.BlockSpec(memory_space=pltpu.SMEM)
PARAMS = pltpu.CompilerParams(vmem_limit_bytes=56 * 1024 * 1024)


def split(x):
    high = x.astype(BF16)
    low = (x - high.astype(F32)).astype(BF16)
    return high, low


def dot(a, b):
    return jnp.dot(a, b, preferred_element_type=F32)


def wide(x):
    high, low = split(x)
    return jnp.concatenate([high, high, low], axis=1)


def tall(x):
    high, low = split(x)
    return jnp.concatenate([high, low, high], axis=0)


def dot3(a, b):
    return dot(wide(a), tall(b))


def identity(n):
    rows = lax.broadcasted_iota(jnp.int32, (n, n), 0)
    cols = lax.broadcasted_iota(jnp.int32, (n, n), 1)
    return (rows == cols).astype(F32)


def factor(a_ref, j_ref):
    n = R
    groups = n // 8
    sub = lax.broadcasted_iota(jnp.int32, (8, n), 0)
    lane = lax.broadcasted_iota(jnp.int32, (8, n), 1)
    rows = [a_ref[8 * g : 8 * g + 8, :] for g in range(groups)]

    def column(x, c):
        return jnp.take_along_axis(x, jnp.full((8, n), c, jnp.int32), axis=1, mode="promise_in_bounds")

    def row(x, r):
        return jnp.broadcast_to(x[r : r + 1, :], (8, n))

    for p in range(groups):
        r0 = 8 * p
        inside = (lane >= r0) & (lane < r0 + 8)
        cols = [column(rows[p], r0 + c) for c in range(8)]
        a = [[row(cols[c], s) for c in range(s + 1)] for s in range(8)]
        panel = jnp.where(inside, (sub == lane - r0).astype(F32), rows[p])
        rs = [None] * 8
        low = [[None] * 8 for _ in range(8)]
        up = [row(panel, r) for r in range(8)]
        later = range(p + 1, groups)
        m = {g: [column(rows[g], r0 + r) for r in range(8)] for g in later}
        acc = {g: jnp.where(inside, 0.0, rows[g]) for g in later}
        for r in range(8):
            rs[r] = lax.rsqrt(a[r][r])
            for s in range(r + 1, 8):
                low[s][r] = a[s][r] * rs[r]
            for s in range(r + 1, 8):
                for c in range(r + 1, s + 1):
                    a[s][c] = a[s][c] - low[s][r] * low[c][r]
            up[r] = up[r] * rs[r]
            for s in range(r + 1, 8):
                up[s] = up[s] - low[s][r] * up[r]
            for g in later:
                m[g][r] = m[g][r] * rs[r]
                for s in range(r + 1, 8):
                    m[g][s] = m[g][s] - low[s][r] * m[g][r]
                acc[g] = acc[g] - m[g][r] * up[r]
        for g in later:
            rows[g] = acc[g]
        done = up[0]
        for r in range(1, 8):
            done = jnp.where(sub == r, up[r], done)
        j_ref[r0 : r0 + 8, :] = jnp.where(lane < r0 + 8, done, 0.0)


def chunks(start, stop, size=256):
    return [(c, min(c + size, stop)) for c in range(start, stop, size)]


def blk(i):
    return slice(i * R, (i + 1) * R)


def leaf_kernel(
    count_ref, xr_ref, xc_ref, basis_ref, rhs_ref,
    t_ref, y_ref, u_ref, li_ref,
    a_ref, j_ref, right_ref, left_ref, yh_ref, yl_ref,
):
    slots, columns = y_ref.shape
    nb = slots // R
    levels = basis_ref.shape[1] // R
    count = count_ref[0]
    live_lane = (lax.broadcasted_iota(jnp.int32, (1, slots), 1) < count).astype(F32)
    live_sub = (lax.broadcasted_iota(jnp.int32, (slots, 1), 0) < count).astype(F32)
    for b in range(nb):
        live_b = live_sub[blk(b), :]
        y_ref[blk(b), : levels * R] = basis_ref[blk(b), :] * live_b
        y_ref[blk(b), levels * R :] = rhs_ref[blk(b), :] * live_b
        for c0, c1 in chunks(b * R, slots, 128):
            dist = None
            for d in range(3):
                diff = xc_ref[blk(b), d : d + 1] - xr_ref[d : d + 1, c0:c1]
                dist = diff * diff if dist is None else dist + diff * diff
            kern = jnp.exp(-GAMMA_RATE * dist) * live_b * live_lane[:, c0:c1]
            if c0 == b * R:
                kern = kern + NUGGET_VALUE * identity(R)
            u_ref[blk(b), c0:c1] = kern

    def step(b, carry):
        here = pl.ds(pl.multiple_of(b * R, R), R)
        a_ref[...] = u_ref[here, here]
        factor(a_ref, j_ref)
        li_ref[here, :] = j_ref[...]
        for static_b in range(nb):

            @pl.when(b == static_b)
            def _(b=static_b):
                inv = wide(j_ref[...])
                for c0, c1 in chunks((b + 1) * R, slots, 256):
                    new = dot(inv, tall(u_ref[blk(b), c0:c1]))
                    u_ref[blk(b), c0:c1] = new
                    right_ref[:, c0:c1] = tall(new)
                    for e0, e1 in chunks(c0, c1, R):
                        left_ref[e0:e1, :] = wide(new[:, e0 - c0 : e1 - c0].T)
                for c0, c1 in chunks(0, columns, 256):
                    new = dot(inv, tall(y_ref[blk(b), c0:c1]))
                    y_ref[blk(b), c0:c1] = new
                    stacked = tall(new)
                    right_ref[:, slots + c0 : slots + c1] = stacked
                    yh_ref[blk(b), c0:c1] = stacked[:R]
                    yl_ref[blk(b), c0:c1] = stacked[R : 2 * R]
                for i in range(b + 1, nb):
                    left = left_ref[blk(i), :]
                    for c0, c1 in chunks(i * R, slots, 256):
                        u_ref[blk(i), c0:c1] = u_ref[blk(i), c0:c1] - dot(left, right_ref[:, c0:c1])
                    for c0, c1 in chunks(0, columns, 256):
                        y_ref[blk(i), c0:c1] = y_ref[blk(i), c0:c1] - dot(
                            left, right_ref[:, slots + c0 : slots + c1]
                        )

        return carry

    lax.fori_loop(0, nb, step, 0)
    offset = 0
    for k in range(levels):
        high, low = split(y_ref[:, blk(k)].T)
        for c0, c1 in chunks(k * R, columns, 256):
            yh = yh_ref[:, c0:c1]
            value = dot(high, yh) + dot(high, yl_ref[:, c0:c1]) + dot(low, yh)
            t_ref[:, offset + c0 - k * R : offset + c1 - k * R] = value
        offset += columns - k * R


def width_of(level, row, levels):
    return sum((levels + 1 - k) * R for k in range(level, row))


def levels_kernel(
    levels, t_ref, e_ref, g_ref,
    own_ref, sib_ref, zt_ref, zl_ref, bd_ref, h_ref, f_ref, eb_ref, et_ref, u_ref, inv_ref, a_ref, j_ref,
    send_sem, recv_sem,
):
    leaf, sub = lax.axis_index("leaf"), lax.axis_index("sub")
    core, z, y = leaf % 2, (leaf // 2) % 4, leaf // 8
    partner = [
        (leaf, sub + 1 - 2 * (sub % 2)),
        (leaf, 3 - sub),
        (leaf + 1 - 2 * core, sub),
        (y * 8 + (z + 1 - 2 * (z % 2)) * 2 + core, sub),
        (y * 8 + (3 - z) * 2 + core, sub),
        ((y + 1 - 2 * (y % 2)) * 8 + z * 2 + core, sub),
        ((3 - y) * 8 + z * 2 + core, sub),
    ]
    position = leaf * 4 + sub
    total = [width_of(k, levels, levels) for k in range(levels)]
    own_base = [0] + [sum(total[1:k]) for k in range(1, levels)]
    sib_base = [sum(total[:k]) for k in range(levels)]
    z_base = [sum((levels - j) * R for j in range(k)) for k in range(levels)]
    first_message = [sum(levels + 1 - j for j in range(k)) for k in range(levels)]

    def span(level, part):
        if part == 0:
            return 0, R
        start = R if part == 1 else width_of(level, level + part - 1, levels)
        return start, width_of(level, level + part, levels) if part > 1 else width_of(level, level + 1, levels)

    def own(level, c0, c1):
        ref = t_ref if level == 0 else own_ref
        return ref.at[:, own_base[level] + c0 : own_base[level] + c1]

    def sib(level, c0, c1):
        return sib_ref.at[:, sib_base[level] + c0 : sib_base[level] + c1]

    def message(level, part):
        c0, c1 = span(level, part)
        index = first_message[level] + part
        return pltpu.make_async_remote_copy(
            src_ref=own(level, c0, c1),
            dst_ref=sib(level, c0, c1),
            send_sem=send_sem.at[index],
            recv_sem=recv_sem.at[index],
            device_id=partner[level],
            device_id_type=pl.DeviceIdType.MESH,
        )

    def side_slices(level):
        side = (position // 2**level) % 2
        mine = pl.ds(pl.multiple_of(side * R, R), R)
        other = pl.ds(pl.multiple_of((1 - side) * R, R), R)
        return mine, other

    def prepare(level):
        e = e_ref[level]
        eb_ref[...] = wide(jnp.concatenate([e[:R].T, e[R:].T], axis=1))
        et_ref[...] = tall(e)

    def begin(level):
        mine, other = side_slices(level)
        bd_ref[mine, other] = jnp.zeros((R, R), F32)
        bd_ref[other, mine] = jnp.zeros((R, R), F32)
        bd_ref[mine, mine] = own(level, 0, R)[...]
        message(level, 0).wait_recv()
        bd_ref[other, other] = sib(level, 0, R)[...]
        x = dot(eb_ref[...], tall(bd_ref[...]))
        h = dot(wide(x), et_ref[...])
        h = 0.5 * (h + h.T)
        a_ref[...] = h[:R, :R] + identity(R)
        h_ref[:R, :] = h[:R, R:]
        h_ref[R:, :] = h[R:, R:]

    def half(level):
        mine, other = side_slices(level)
        inverse = j_ref[...]
        inv_ref[...] = inverse
        stacked = wide(inverse)
        upper = dot(stacked, tall(h_ref[:R, :]))
        ut = upper.T
        u_ref[...] = upper
        left = wide(ut)
        a_ref[...] = h_ref[R:, :] + identity(R) - dot(left, tall(upper))
        message(level, 1).wait_recv()
        w = (levels - level) * R
        f_ref[mine, :w] = own(level, R, R + w)[...]
        f_ref[other, :w] = sib(level, R, R + w)[...]
        zb = z_base[level]
        for c0, c1 in chunks(0, w):
            forcing = dot(eb_ref[...], tall(f_ref[:, c0:c1]))
            z1 = dot(stacked, tall(forcing[:R]))
            f_ref[:R, c0:c1] = z1
            f_ref[R:, c0:c1] = forcing[R:] - dot(left, tall(z1))

    def finish(level):
        w = (levels - level) * R
        zb = z_base[level]
        stacked = wide(j_ref[...])
        for c0, c1 in chunks(0, w):
            f_ref[R:, c0:c1] = dot(stacked, tall(f_ref[R:, c0:c1]))
            value = f_ref[:, c0:c1]
            zt_ref[:, zb + c0 : zb + c1] = tall(value)
            zl_ref[zb + c0 : zb + c1, :] = wide(value.T)

    def update(level, row):
        part = row - level + 1
        message(level, part).wait_recv()
        c0, c1 = span(level, part)
        n0 = width_of(level + 1, row, levels)
        zb = z_base[level]
        shift = (row - level - 1) * R
        left = zl_ref[zb + shift : zb + shift + R, :]
        for d0, d1 in chunks(0, c1 - c0):
            value = own(level, c0 + d0, c0 + d1)[...] + sib(level, c0 + d0, c0 + d1)[...]
            value = value - dot(left, zt_ref[:, zb + shift + d0 : zb + shift + d1])
            own(level + 1, n0 + d0, n0 + d1)[...] = value
        if row == level + 1:
            message(level + 1, 0).start()
            message(level + 1, 1).start()
        else:
            message(level + 1, row - level).start()

    def gains(level):
        mine, _ = side_slices(level)
        e_own = e_ref[level, mine, :]
        w1 = dot3(e_own[:, :R], inv_ref[...].T)
        w2 = dot3(e_own[:, R:] - dot3(w1, u_ref[...]), j_ref[...].T)
        w = wide(jnp.concatenate([w1, w2], axis=1))
        zb = z_base[level]
        for c0, c1 in chunks(0, (levels - level) * R):
            g_ref[:, zb + c0 : zb + c1] = dot(w, zt_ref[:, zb + c0 : zb + c1])

    barrier = pltpu.get_barrier_semaphore()
    for device in partner:
        pl.semaphore_signal(barrier, inc=1, device_id=device, device_id_type=pl.DeviceIdType.MESH)
    pl.semaphore_wait(barrier, levels)
    for part in range(levels + 1):
        message(0, part).start()
    prepare(0)
    begin(0)

    late = {
        (1, 0): [(0, 2)],
        (1, 1): [(0, 3)],
        (2, 0): [(0, 4), (0, 5)],
        (2, 1): [(0, 6), (1, 3)],
        (3, 0): [(1, 4), (1, 5), (1, 6), (2, 4)],
        (4, 0): [(2, 5), (2, 6), (3, 5), (3, 6)],
        (5, 0): [(4, 6)],
    }

    def step(i, carry):
        factor(a_ref, j_ref)
        for level in range(levels):

            @pl.when(i == 2 * level)
            def _(level=level):
                half(level)
                for pair in late.get((level, 0), []):
                    update(*pair)

            @pl.when(i == 2 * level + 1)
            def _(level=level):
                finish(level)
                for pair in late.get((level, 1), []):
                    update(*pair)
                if level < levels - 1:
                    update(level, level + 1)
                    prepare(level + 1)
                gains(level)
                if level < levels - 1:
                    begin(level + 1)

        return carry

    lax.fori_loop(0, 2 * levels, step, 0)
    for level in range(levels):
        for part in range(levels + 1 - level):
            message(level, part).wait_send()


def final_kernel(y_ref, u_ref, li_ref, g_ref, out_ref, v_ref, x_ref):
    levels = y_ref.shape[1] // R - 1
    slots = y_ref.shape[0]
    nb = slots // R
    for k in reversed(range(levels)):
        base = sum((levels - j) * R for j in range(k))
        inner = (levels - 1 - k) * R
        value = -g_ref[:, base + inner : base + inner + R]
        if inner > 0:
            value = value - dot3(g_ref[:, base : base + inner], v_ref[(k + 1) * R :, :])
        v_ref[blk(k), :] = value
    vt = tall(v_ref[...])
    for b in range(nb):
        x_ref[blk(b), :] = y_ref[blk(b), levels * R :] + dot(wide(y_ref[blk(b), : levels * R]), vt)
    for b in reversed(range(nb)):
        value = dot3(li_ref[blk(b), :].T, x_ref[blk(b), :])
        out_ref[blk(b), :] = value
        if b > 0:
            x_ref[: b * R, :] = x_ref[: b * R, :] - dot3(u_ref[: b * R, blk(b)], value)


def f32(*shape):
    return jax.ShapeDtypeStruct(shape, F32)


def call(kernel, outs, ins, scratch=(), params=PARAMS, **kw):
    return pl.pallas_call(
        kernel,
        out_shape=outs,
        in_specs=ins,
        out_specs=jax.tree.map(lambda _: VMEM, outs),
        scratch_shapes=list(scratch),
        compiler_params=params,
        **kw,
    )


def shards(points, order, counts, basis, right_side, coupling):
    slots = points.shape[1]
    levels = basis.shape[1] // R
    columns = levels * R + right_side.shape[1]
    ordered = points[:, order[0]]
    packed = width_of(0, levels, levels)
    t, y, u, li = call(
        leaf_kernel,
        (f32(R, packed), f32(slots, columns), f32(slots, slots), f32(slots, R)),
        [SMEM, VMEM, VMEM, VMEM, VMEM],
        [
            pltpu.VMEM((R, R), F32),
            pltpu.VMEM((R, R), F32),
            pltpu.VMEM((3 * R, slots + columns), BF16),
            pltpu.VMEM((slots, 3 * R), BF16),
            pltpu.VMEM((slots, columns), BF16),
            pltpu.VMEM((slots, columns), BF16),
        ],
    )(counts, ordered, ordered.T, basis, right_side)
    own_width = sum(width_of(k, levels, levels) for k in range(1, levels))
    gain_width = sum((levels - k) * R for k in range(levels))
    messages = sum(levels + 1 - k for k in range(levels))
    g = call(
        functools.partial(levels_kernel, levels),
        f32(R, gain_width),
        [VMEM, VMEM],
        [
            pltpu.VMEM((R, own_width), F32),
            pltpu.VMEM((R, own_width + packed), F32),
            pltpu.VMEM((6 * R, gain_width), BF16),
            pltpu.VMEM((gain_width, 6 * R), BF16),
            pltpu.VMEM((2 * R, 2 * R), F32),
            pltpu.VMEM((2 * R, R), F32),
            pltpu.VMEM((2 * R, levels * R), F32),
            pltpu.VMEM((2 * R, 6 * R), BF16),
            pltpu.VMEM((6 * R, 2 * R), BF16),
            pltpu.VMEM((R, R), F32),
            pltpu.VMEM((R, R), F32),
            pltpu.VMEM((R, R), F32),
            pltpu.VMEM((R, R), F32),
            pltpu.SemaphoreType.DMA((messages,)),
            pltpu.SemaphoreType.DMA((messages,)),
        ],
        pltpu.CompilerParams(
            vmem_limit_bytes=56 * 1024 * 1024, collective_id=0, has_side_effects=True
        ),
    )(t, coupling)
    return call(
        final_kernel,
        f32(slots, columns - levels * R),
        [VMEM] * 4,
        [pltpu.VMEM((levels * R, R), F32), pltpu.VMEM((slots, R), F32)],
    )(y, u, li, g)


def solution(mesh):
    placed = (
        P(None, ("leaf", "sub")),
        P(("leaf", "sub"), None),
        P(("leaf", "sub")),
        P(("leaf", "sub"), None),
        P(("leaf", "sub"), None),
        P(),
    )
    return jax.shard_map(
        shards, mesh=mesh, in_specs=placed, out_specs=P(("leaf", "sub"), None), check_vma=False
    )
```

```python
import functools

import jax
import jax.numpy as jnp
from jax import lax
from jax.experimental import pallas as pl
from jax.experimental.pallas import tpu as pltpu
from jax.sharding import PartitionSpec as P

R = 128
GAMMA_RATE = 2.0
NUGGET_VALUE = 1.0
F32 = jnp.float32
BF16 = jnp.bfloat16
VMEM = pl.BlockSpec(memory_space=pltpu.VMEM)
SMEM = pl.BlockSpec(memory_space=pltpu.SMEM)
PARAMS = pltpu.CompilerParams(vmem_limit_bytes=56 * 1024 * 1024)


def split(x):
    high = x.astype(BF16)
    low = (x - high.astype(F32)).astype(BF16)
    return high, low


def dot(a, b):
    return jnp.dot(a, b, preferred_element_type=F32)


def wide(x):
    high, low = split(x)
    return jnp.concatenate([high, high, low], axis=1)


def tall(x):
    high, low = split(x)
    return jnp.concatenate([high, low, high], axis=0)


def dot3(a, b):
    return dot(wide(a), tall(b))


def identity(n):
    rows = lax.broadcasted_iota(jnp.int32, (n, n), 0)
    cols = lax.broadcasted_iota(jnp.int32, (n, n), 1)
    return (rows == cols).astype(F32)


def factor(a_ref, j_ref):
    n = R
    groups = n // 8
    sub = lax.broadcasted_iota(jnp.int32, (8, n), 0)
    lane = lax.broadcasted_iota(jnp.int32, (8, n), 1)
    rows = [a_ref[8 * g : 8 * g + 8, :] for g in range(groups)]

    def column(x, c):
        return jnp.take_along_axis(x, jnp.full((8, n), c, jnp.int32), axis=1, mode="promise_in_bounds")

    def row(x, r):
        return jnp.broadcast_to(x[r : r + 1, :], (8, n))

    for p in range(groups):
        r0 = 8 * p
        inside = (lane >= r0) & (lane < r0 + 8)
        cols = [column(rows[p], r0 + c) for c in range(8)]
        a = [[row(cols[c], s) for c in range(s + 1)] for s in range(8)]
        panel = jnp.where(inside, (sub == lane - r0).astype(F32), rows[p])
        rs = [None] * 8
        low = [[None] * 8 for _ in range(8)]
        up = [row(panel, r) for r in range(8)]
        later = range(p + 1, groups)
        m = {g: [column(rows[g], r0 + r) for r in range(8)] for g in later}
        acc = {g: jnp.where(inside, 0.0, rows[g]) for g in later}
        for r in range(8):
            rs[r] = lax.rsqrt(a[r][r])
            for s in range(r + 1, 8):
                low[s][r] = a[s][r] * rs[r]
            for s in range(r + 1, 8):
                for c in range(r + 1, s + 1):
                    a[s][c] = a[s][c] - low[s][r] * low[c][r]
            up[r] = up[r] * rs[r]
            for s in range(r + 1, 8):
                up[s] = up[s] - low[s][r] * up[r]
            for g in later:
                m[g][r] = m[g][r] * rs[r]
                for s in range(r + 1, 8):
                    m[g][s] = m[g][s] - low[s][r] * m[g][r]
                acc[g] = acc[g] - m[g][r] * up[r]
        for g in later:
            rows[g] = acc[g]
        done = up[0]
        for r in range(1, 8):
            done = jnp.where(sub == r, up[r], done)
        j_ref[r0 : r0 + 8, :] = jnp.where(lane < r0 + 8, done, 0.0)


def chunks(start, stop, size=256):
    return [(c, min(c + size, stop)) for c in range(start, stop, size)]


def blk(i):
    return slice(i * R, (i + 1) * R)


def leaf_kernel(
    count_ref, points_ref, order_ref, basis_ref, rhs_ref,
    t_ref, y_ref, u_ref, li_ref,
    a_ref, j_ref, right_ref, left_ref, yh_ref, yl_ref, xr_ref, xc_ref,
):
    slots, columns = y_ref.shape
    nb = slots // R
    levels = basis_ref.shape[1] // R
    count = count_ref[0]
    points = points_ref[...]
    high = points.astype(BF16)
    middle = (points - high.astype(F32)).astype(BF16)
    low = (points - high.astype(F32) - middle.astype(F32)).astype(BF16)
    xr_ref[...] = jnp.zeros_like(xr_ref)
    source = lax.broadcasted_iota(jnp.int32, (slots, 256), 0)
    for c0, c1 in chunks(0, slots, 256):
        chosen = (source == order_ref[:, c0:c1]).astype(F32).astype(BF16)
        xr_ref[:3, c0:c1] = dot(high, chosen) + dot(middle, chosen) + dot(low, chosen)
    for b in range(nb):
        xc_ref[blk(b), :] = xr_ref[:, blk(b)].T
    live_lane = (lax.broadcasted_iota(jnp.int32, (1, slots), 1) < count).astype(F32)
    live_sub = (lax.broadcasted_iota(jnp.int32, (slots, 1), 0) < count).astype(F32)
    for b in range(nb):
        live_b = live_sub[blk(b), :]
        y_ref[blk(b), : levels * R] = basis_ref[blk(b), :] * live_b
        y_ref[blk(b), levels * R :] = rhs_ref[blk(b), :] * live_b
        for c0, c1 in chunks(b * R, slots, 128):
            dist = None
            for d in range(3):
                diff = xc_ref[blk(b), d : d + 1] - xr_ref[d : d + 1, c0:c1]
                dist = diff * diff if dist is None else dist + diff * diff
            kern = jnp.exp(-GAMMA_RATE * dist) * live_b * live_lane[:, c0:c1]
            if c0 == b * R:
                kern = kern + NUGGET_VALUE * identity(R)
            u_ref[blk(b), c0:c1] = kern

    def step(b, carry):
        here = pl.ds(pl.multiple_of(b * R, R), R)
        a_ref[...] = u_ref[here, here]
        factor(a_ref, j_ref)
        li_ref[here, :] = j_ref[...]
        for static_b in range(nb):

            @pl.when(b == static_b)
            def _(b=static_b):
                inv = wide(j_ref[...])
                for c0, c1 in chunks((b + 1) * R, slots, 256):
                    new = dot(inv, tall(u_ref[blk(b), c0:c1]))
                    u_ref[blk(b), c0:c1] = new
                    right_ref[:, c0:c1] = tall(new)
                    for e0, e1 in chunks(c0, c1, R):
                        left_ref[e0:e1, :] = wide(new[:, e0 - c0 : e1 - c0].T)
                for c0, c1 in chunks(0, columns, 256):
                    new = dot(inv, tall(y_ref[blk(b), c0:c1]))
                    y_ref[blk(b), c0:c1] = new
                    stacked = tall(new)
                    right_ref[:, slots + c0 : slots + c1] = stacked
                    yh_ref[blk(b), c0:c1] = stacked[:R]
                    yl_ref[blk(b), c0:c1] = stacked[R : 2 * R]
                for i in range(b + 1, nb):
                    left = left_ref[blk(i), :]
                    for c0, c1 in chunks(i * R, slots, 256):
                        u_ref[blk(i), c0:c1] = u_ref[blk(i), c0:c1] - dot(left, right_ref[:, c0:c1])
                    for c0, c1 in chunks(0, columns, 256):
                        y_ref[blk(i), c0:c1] = y_ref[blk(i), c0:c1] - dot(
                            left, right_ref[:, slots + c0 : slots + c1]
                        )

        return carry

    lax.fori_loop(0, nb, step, 0)
    offset = 0
    for k in range(levels):
        high, low = split(y_ref[:, blk(k)].T)
        for c0, c1 in chunks(k * R, columns, 256):
            yh = yh_ref[:, c0:c1]
            value = dot(high, yh) + dot(high, yl_ref[:, c0:c1]) + dot(low, yh)
            t_ref[:, offset + c0 - k * R : offset + c1 - k * R] = value
        offset += columns - k * R


def width_of(level, row, levels):
    return sum((levels + 1 - k) * R for k in range(level, row))


def levels_kernel(
    levels, t_ref, e_ref, g_ref,
    own_ref, sib_ref, zt_ref, zl_ref, bd_ref, h_ref, f_ref, eb_ref, et_ref, u_ref, inv_ref, a_ref, j_ref,
    send_sem, recv_sem,
):
    leaf, sub = lax.axis_index("leaf"), lax.axis_index("sub")
    core, z, y = leaf % 2, (leaf // 2) % 4, leaf // 8
    partner = [
        (leaf, sub + 1 - 2 * (sub % 2)),
        (leaf, 3 - sub),
        (leaf + 1 - 2 * core, sub),
        (y * 8 + (z + 1 - 2 * (z % 2)) * 2 + core, sub),
        (y * 8 + (3 - z) * 2 + core, sub),
        ((y + 1 - 2 * (y % 2)) * 8 + z * 2 + core, sub),
        ((3 - y) * 8 + z * 2 + core, sub),
    ]
    position = leaf * 4 + sub
    total = [width_of(k, levels, levels) for k in range(levels)]
    own_base = [0] + [sum(total[1:k]) for k in range(1, levels)]
    sib_base = [sum(total[:k]) for k in range(levels)]
    z_base = [sum((levels - j) * R for j in range(k)) for k in range(levels)]
    first_message = [sum(levels + 1 - j for j in range(k)) for k in range(levels)]

    def span(level, part):
        if part == 0:
            return 0, R
        start = R if part == 1 else width_of(level, level + part - 1, levels)
        return start, width_of(level, level + part, levels) if part > 1 else width_of(level, level + 1, levels)

    def own(level, c0, c1):
        ref = t_ref if level == 0 else own_ref
        return ref.at[:, own_base[level] + c0 : own_base[level] + c1]

    def sib(level, c0, c1):
        return sib_ref.at[:, sib_base[level] + c0 : sib_base[level] + c1]

    def message(level, part):
        c0, c1 = span(level, part)
        index = first_message[level] + part
        return pltpu.make_async_remote_copy(
            src_ref=own(level, c0, c1),
            dst_ref=sib(level, c0, c1),
            send_sem=send_sem.at[index],
            recv_sem=recv_sem.at[index],
            device_id=partner[level],
            device_id_type=pl.DeviceIdType.MESH,
        )

    def side_slices(level):
        side = (position // 2**level) % 2
        mine = pl.ds(pl.multiple_of(side * R, R), R)
        other = pl.ds(pl.multiple_of((1 - side) * R, R), R)
        return mine, other

    def prepare(level):
        e = e_ref[level]
        eb_ref[...] = wide(jnp.concatenate([e[:R].T, e[R:].T], axis=1))
        et_ref[...] = tall(e)

    def begin(level):
        mine, other = side_slices(level)
        bd_ref[mine, other] = jnp.zeros((R, R), F32)
        bd_ref[other, mine] = jnp.zeros((R, R), F32)
        bd_ref[mine, mine] = own(level, 0, R)[...]
        message(level, 0).wait_recv()
        bd_ref[other, other] = sib(level, 0, R)[...]
        x = dot(eb_ref[...], tall(bd_ref[...]))
        h = dot(wide(x), et_ref[...])
        h = 0.5 * (h + h.T)
        a_ref[...] = h[:R, :R] + identity(R)
        h_ref[:R, :] = h[:R, R:]
        h_ref[R:, :] = h[R:, R:]

    def half(level):
        mine, other = side_slices(level)
        inverse = j_ref[...]
        inv_ref[...] = inverse
        stacked = wide(inverse)
        upper = dot(stacked, tall(h_ref[:R, :]))
        ut = upper.T
        u_ref[...] = upper
        left = wide(ut)
        a_ref[...] = h_ref[R:, :] + identity(R) - dot(left, tall(upper))
        message(level, 1).wait_recv()
        w = (levels - level) * R
        f_ref[mine, :w] = own(level, R, R + w)[...]
        f_ref[other, :w] = sib(level, R, R + w)[...]
        zb = z_base[level]
        for c0, c1 in chunks(0, w):
            forcing = dot(eb_ref[...], tall(f_ref[:, c0:c1]))
            z1 = dot(stacked, tall(forcing[:R]))
            f_ref[:R, c0:c1] = z1
            f_ref[R:, c0:c1] = forcing[R:] - dot(left, tall(z1))

    def finish(level):
        w = (levels - level) * R
        zb = z_base[level]
        stacked = wide(j_ref[...])
        for c0, c1 in chunks(0, w):
            f_ref[R:, c0:c1] = dot(stacked, tall(f_ref[R:, c0:c1]))
            value = f_ref[:, c0:c1]
            zt_ref[:, zb + c0 : zb + c1] = tall(value)
            zl_ref[zb + c0 : zb + c1, :] = wide(value.T)

    def update(level, row):
        part = row - level + 1
        message(level, part).wait_recv()
        c0, c1 = span(level, part)
        n0 = width_of(level + 1, row, levels)
        zb = z_base[level]
        shift = (row - level - 1) * R
        left = zl_ref[zb + shift : zb + shift + R, :]
        for d0, d1 in chunks(0, c1 - c0):
            value = own(level, c0 + d0, c0 + d1)[...] + sib(level, c0 + d0, c0 + d1)[...]
            value = value - dot(left, zt_ref[:, zb + shift + d0 : zb + shift + d1])
            own(level + 1, n0 + d0, n0 + d1)[...] = value
        if row == level + 1:
            message(level + 1, 0).start()
            message(level + 1, 1).start()
        else:
            message(level + 1, row - level).start()

    def gains(level):
        mine, _ = side_slices(level)
        e_own = e_ref[level, mine, :]
        w1 = dot3(e_own[:, :R], inv_ref[...].T)
        w2 = dot3(e_own[:, R:] - dot3(w1, u_ref[...]), j_ref[...].T)
        w = wide(jnp.concatenate([w1, w2], axis=1))
        zb = z_base[level]
        for c0, c1 in chunks(0, (levels - level) * R):
            g_ref[:, zb + c0 : zb + c1] = dot(w, zt_ref[:, zb + c0 : zb + c1])

    barrier = pltpu.get_barrier_semaphore()
    for device in partner:
        pl.semaphore_signal(barrier, inc=1, device_id=device, device_id_type=pl.DeviceIdType.MESH)
    pl.semaphore_wait(barrier, levels)
    message(0, 0).start()
    message(0, 1).start()
    prepare(0)
    begin(0)

    starts = {(0, 0): [2], (0, 1): [3], (1, 0): [4], (1, 1): [5, 6, 7]}
    ahead = {(1, 0): [(0, 2)], (3, 0): [(2, 4)]}
    after = {
        (2, 0): [(0, 4)],
        (2, 1): [(1, 3), (0, 5), (0, 6)],
        (3, 0): [(1, 5), (1, 6)],
        (4, 0): [(3, 5), (3, 6)],
        (5, 0): [(4, 6)],
    }
    then = {(1, 1): [(0, 3)], (2, 1): [(1, 4)], (3, 1): [(2, 5), (2, 6)]}

    def step(i, carry):
        factor(a_ref, j_ref)
        for level in range(levels):

            @pl.when(i == 2 * level)
            def _(level=level):
                for part in starts.get((level, 0), []):
                    message(0, part).start()
                for pair in ahead.get((level, 0), []):
                    update(*pair)
                half(level)
                for pair in after.get((level, 0), []):
                    update(*pair)

            @pl.when(i == 2 * level + 1)
            def _(level=level):
                for part in starts.get((level, 1), []):
                    message(0, part).start()
                finish(level)
                for pair in after.get((level, 1), []):
                    update(*pair)
                if level < levels - 1:
                    update(level, level + 1)
                    for pair in then.get((level, 1), []):
                        update(*pair)
                    prepare(level + 1)
                gains(level)
                if level < levels - 1:
                    begin(level + 1)

        return carry

    lax.fori_loop(0, 2 * levels, step, 0)
    for level in range(levels):
        for part in range(levels + 1 - level):
            message(level, part).wait_send()


def final_kernel(y_ref, u_ref, li_ref, g_ref, out_ref, v_ref, x_ref):
    levels = y_ref.shape[1] // R - 1
    slots = y_ref.shape[0]
    nb = slots // R
    for k in reversed(range(levels)):
        base = sum((levels - j) * R for j in range(k))
        inner = (levels - 1 - k) * R
        value = -g_ref[:, base + inner : base + inner + R]
        if inner > 0:
            value = value - dot3(g_ref[:, base : base + inner], v_ref[(k + 1) * R :, :])
        v_ref[blk(k), :] = value
    vt = tall(v_ref[...])
    for b in range(nb):
        x_ref[blk(b), :] = y_ref[blk(b), levels * R :] + dot(wide(y_ref[blk(b), : levels * R]), vt)
    for b in reversed(range(nb)):
        value = dot3(li_ref[blk(b), :].T, x_ref[blk(b), :])
        out_ref[blk(b), :] = value
        if b > 0:
            x_ref[: b * R, :] = x_ref[: b * R, :] - dot3(u_ref[: b * R, blk(b)], value)


def f32(*shape):
    return jax.ShapeDtypeStruct(shape, F32)


def call(kernel, outs, ins, scratch=(), params=PARAMS, **kw):
    return pl.pallas_call(
        kernel,
        out_shape=outs,
        in_specs=ins,
        out_specs=jax.tree.map(lambda _: VMEM, outs),
        scratch_shapes=list(scratch),
        compiler_params=params,
        **kw,
    )


def shards(points, order, counts, basis, right_side, coupling):
    slots = points.shape[1]
    levels = basis.shape[1] // R
    columns = levels * R + right_side.shape[1]
    packed = width_of(0, levels, levels)
    t, y, u, li = call(
        leaf_kernel,
        (f32(R, packed), f32(slots, columns), f32(slots, slots), f32(slots, R)),
        [SMEM, VMEM, VMEM, VMEM, VMEM],
        [
            pltpu.VMEM((R, R), F32),
            pltpu.VMEM((R, R), F32),
            pltpu.VMEM((3 * R, slots + columns), BF16),
            pltpu.VMEM((slots, 3 * R), BF16),
            pltpu.VMEM((slots, columns), BF16),
            pltpu.VMEM((slots, columns), BF16),
            pltpu.VMEM((8, slots), F32),
            pltpu.VMEM((slots, 8), F32),
        ],
    )(counts, points, order, basis, right_side)
    own_width = sum(width_of(k, levels, levels) for k in range(1, levels))
    gain_width = sum((levels - k) * R for k in range(levels))
    messages = sum(levels + 1 - k for k in range(levels))
    g = call(
        functools.partial(levels_kernel, levels),
        f32(R, gain_width),
        [VMEM, VMEM],
        [
            pltpu.VMEM((R, own_width), F32),
            pltpu.VMEM((R, own_width + packed), F32),
            pltpu.VMEM((6 * R, gain_width), BF16),
            pltpu.VMEM((gain_width, 6 * R), BF16),
            pltpu.VMEM((2 * R, 2 * R), F32),
            pltpu.VMEM((2 * R, R), F32),
            pltpu.VMEM((2 * R, levels * R), F32),
            pltpu.VMEM((2 * R, 6 * R), BF16),
            pltpu.VMEM((6 * R, 2 * R), BF16),
            pltpu.VMEM((R, R), F32),
            pltpu.VMEM((R, R), F32),
            pltpu.VMEM((R, R), F32),
            pltpu.VMEM((R, R), F32),
            pltpu.SemaphoreType.DMA((messages,)),
            pltpu.SemaphoreType.DMA((messages,)),
        ],
        pltpu.CompilerParams(
            vmem_limit_bytes=56 * 1024 * 1024, collective_id=0, has_side_effects=True
        ),
    )(t, coupling)
    return call(
        final_kernel,
        f32(slots, columns - levels * R),
        [VMEM] * 4,
        [pltpu.VMEM((levels * R, R), F32), pltpu.VMEM((slots, R), F32)],
    )(y, u, li, g)


def solution(mesh):
    placed = (
        P(None, ("leaf", "sub")),
        P(("leaf", "sub"), None),
        P(("leaf", "sub")),
        P(("leaf", "sub"), None),
        P(("leaf", "sub"), None),
        P(),
    )
    return jax.shard_map(
        shards, mesh=mesh, in_specs=placed, out_specs=P(("leaf", "sub"), None), check_vma=False
    )
```

```python
import functools

import jax
import jax.numpy as jnp
from jax import lax
from jax.experimental import pallas as pl
from jax.experimental.pallas import tpu as pltpu
from jax.sharding import PartitionSpec as P

R = 128
GAMMA_RATE = 2.0
NUGGET_VALUE = 1.0
F32 = jnp.float32
BF16 = jnp.bfloat16
VMEM = pl.BlockSpec(memory_space=pltpu.VMEM)
SMEM = pl.BlockSpec(memory_space=pltpu.SMEM)
ANY = pl.BlockSpec(memory_space=pl.ANY)
PARAMS = pltpu.CompilerParams(vmem_limit_bytes=56 * 1024 * 1024)


def split(x):
    high = x.astype(BF16)
    low = (x - high.astype(F32)).astype(BF16)
    return high, low


def dot(a, b):
    return jnp.dot(a, b, preferred_element_type=F32)


def wide(x):
    high, low = split(x)
    return jnp.concatenate([high, high, low], axis=1)


def tall(x):
    high, low = split(x)
    return jnp.concatenate([high, low, high], axis=0)


def dot3(a, b):
    return dot(wide(a), tall(b))


def identity(n):
    rows = lax.broadcasted_iota(jnp.int32, (n, n), 0)
    cols = lax.broadcasted_iota(jnp.int32, (n, n), 1)
    return (rows == cols).astype(F32)


def factor(a_ref, j_ref):
    n = R
    groups = n // 8
    sub = lax.broadcasted_iota(jnp.int32, (8, n), 0)
    lane = lax.broadcasted_iota(jnp.int32, (8, n), 1)
    rows = [a_ref[8 * g : 8 * g + 8, :] for g in range(groups)]

    def column(x, c):
        return jnp.take_along_axis(x, jnp.full((8, n), c, jnp.int32), axis=1, mode="promise_in_bounds")

    def row(x, r):
        return jnp.broadcast_to(x[r : r + 1, :], (8, n))

    for p in range(groups):
        r0 = 8 * p
        inside = (lane >= r0) & (lane < r0 + 8)
        cols = [column(rows[p], r0 + c) for c in range(8)]
        a = [[row(cols[c], s) for c in range(s + 1)] for s in range(8)]
        panel = jnp.where(inside, (sub == lane - r0).astype(F32), rows[p])
        rs = [None] * 8
        low = [[None] * 8 for _ in range(8)]
        up = [row(panel, r) for r in range(8)]
        later = range(p + 1, groups)
        m = {g: [column(rows[g], r0 + r) for r in range(8)] for g in later}
        acc = {g: jnp.where(inside, 0.0, rows[g]) for g in later}
        for r in range(8):
            rs[r] = lax.rsqrt(a[r][r])
            for s in range(r + 1, 8):
                low[s][r] = a[s][r] * rs[r]
            for s in range(r + 1, 8):
                for c in range(r + 1, s + 1):
                    a[s][c] = a[s][c] - low[s][r] * low[c][r]
            up[r] = up[r] * rs[r]
            for s in range(r + 1, 8):
                up[s] = up[s] - low[s][r] * up[r]
            for g in later:
                m[g][r] = m[g][r] * rs[r]
                for s in range(r + 1, 8):
                    m[g][s] = m[g][s] - low[s][r] * m[g][r]
                acc[g] = acc[g] - m[g][r] * up[r]
        for g in later:
            rows[g] = acc[g]
        done = up[0]
        for r in range(1, 8):
            done = jnp.where(sub == r, up[r], done)
        j_ref[r0 : r0 + 8, :] = jnp.where(lane < r0 + 8, done, 0.0)


def chunks(start, stop, size=256):
    return [(c, min(c + size, stop)) for c in range(start, stop, size)]


def blk(i):
    return slice(i * R, (i + 1) * R)


def leaf_kernel(
    count_ref, points_ref, order_ref, basis_ref, rhs_ref,
    t_ref, y_ref, u_ref, li_ref,
    a_ref, j_ref, right_ref, left_ref, yh_ref, yl_ref, xr_ref, xc_ref,
):
    slots, columns = y_ref.shape
    nb = slots // R
    levels = basis_ref.shape[1] // R
    count = count_ref[0]
    points = points_ref[...]
    high = points.astype(BF16)
    middle = (points - high.astype(F32)).astype(BF16)
    low = (points - high.astype(F32) - middle.astype(F32)).astype(BF16)
    xr_ref[...] = jnp.zeros_like(xr_ref)
    source = lax.broadcasted_iota(jnp.int32, (slots, 256), 0)
    for c0, c1 in chunks(0, slots, 256):
        chosen = (source == order_ref[:, c0:c1]).astype(F32).astype(BF16)
        xr_ref[:3, c0:c1] = dot(high, chosen) + dot(middle, chosen) + dot(low, chosen)
    for b in range(nb):
        xc_ref[blk(b), :] = xr_ref[:, blk(b)].T
    live_lane = (lax.broadcasted_iota(jnp.int32, (1, slots), 1) < count).astype(F32)
    live_sub = (lax.broadcasted_iota(jnp.int32, (slots, 1), 0) < count).astype(F32)
    for b in range(nb):
        live_b = live_sub[blk(b), :]
        y_ref[blk(b), : levels * R] = basis_ref[blk(b), :] * live_b
        y_ref[blk(b), levels * R :] = rhs_ref[blk(b), :] * live_b
        for c0, c1 in chunks(b * R, slots, 128):
            dist = None
            for d in range(3):
                diff = xc_ref[blk(b), d : d + 1] - xr_ref[d : d + 1, c0:c1]
                dist = diff * diff if dist is None else dist + diff * diff
            kern = jnp.exp(-GAMMA_RATE * dist) * live_b * live_lane[:, c0:c1]
            if c0 == b * R:
                kern = kern + NUGGET_VALUE * identity(R)
            u_ref[blk(b), c0:c1] = kern

    def step(b, carry):
        here = pl.ds(pl.multiple_of(b * R, R), R)
        a_ref[...] = u_ref[here, here]
        factor(a_ref, j_ref)
        li_ref[here, :] = j_ref[...]
        for static_b in range(nb):

            @pl.when(b == static_b)
            def _(b=static_b):
                inv = wide(j_ref[...])
                for c0, c1 in chunks((b + 1) * R, slots, 256):
                    new = dot(inv, tall(u_ref[blk(b), c0:c1]))
                    u_ref[blk(b), c0:c1] = new
                    right_ref[:, c0:c1] = tall(new)
                    for e0, e1 in chunks(c0, c1, R):
                        left_ref[e0:e1, :] = wide(new[:, e0 - c0 : e1 - c0].T)
                for c0, c1 in chunks(0, columns, 256):
                    new = dot(inv, tall(y_ref[blk(b), c0:c1]))
                    y_ref[blk(b), c0:c1] = new
                    stacked = tall(new)
                    right_ref[:, slots + c0 : slots + c1] = stacked
                    yh_ref[blk(b), c0:c1] = stacked[:R]
                    yl_ref[blk(b), c0:c1] = stacked[R : 2 * R]
                for i in range(b + 1, nb):
                    left = left_ref[blk(i), :]
                    for c0, c1 in chunks(i * R, slots, 256):
                        u_ref[blk(i), c0:c1] = u_ref[blk(i), c0:c1] - dot(left, right_ref[:, c0:c1])
                    for c0, c1 in chunks(0, columns, 256):
                        y_ref[blk(i), c0:c1] = y_ref[blk(i), c0:c1] - dot(
                            left, right_ref[:, slots + c0 : slots + c1]
                        )

        return carry

    lax.fori_loop(0, nb, step, 0)
    project(0, 0, y_ref, yh_ref, yl_ref, t_ref)


def project(k, offset, y_ref, yh_ref, yl_ref, t_ref):
    columns = y_ref.shape[1]
    high, low = split(y_ref[:, blk(k)].T)
    for c0, c1 in chunks(k * R, columns, 256):
        yh = yh_ref[:, c0:c1]
        value = dot(high, yh) + dot(high, yl_ref[:, c0:c1]) + dot(low, yh)
        t_ref[:, offset + c0 - k * R : offset + c1 - k * R] = value


def width_of(level, row, levels):
    return sum((levels + 1 - k) * R for k in range(level, row))


def levels_kernel(
    levels, row_ref, y_hbm, e_ref, g_ref,
    t_ref, y_ref, yh_ref, yl_ref, own_ref, sib_ref, zt_ref, zl_ref, bd_ref, h_ref, f_ref, eb_ref, et_ref, u_ref, inv_ref, a_ref, j_ref,
    send_sem, recv_sem, y_sem,
):
    fetch = pltpu.make_async_copy(y_hbm, y_ref, y_sem)
    fetch.start()
    row_width = row_ref.shape[1]
    leaf, sub = lax.axis_index("leaf"), lax.axis_index("sub")
    core, z, y = leaf % 2, (leaf // 2) % 4, leaf // 8
    partner = [
        (leaf, sub + 1 - 2 * (sub % 2)),
        (leaf, 3 - sub),
        (leaf + 1 - 2 * core, sub),
        (y * 8 + (z + 1 - 2 * (z % 2)) * 2 + core, sub),
        (y * 8 + (3 - z) * 2 + core, sub),
        ((y + 1 - 2 * (y % 2)) * 8 + z * 2 + core, sub),
        ((3 - y) * 8 + z * 2 + core, sub),
    ]
    position = leaf * 4 + sub
    total = [width_of(k, levels, levels) for k in range(levels)]
    own_base = [0] + [sum(total[1:k]) for k in range(1, levels)]
    sib_base = [sum(total[:k]) for k in range(levels)]
    z_base = [sum((levels - j) * R for j in range(k)) for k in range(levels)]
    first_message = [sum(levels + 1 - j for j in range(k)) for k in range(levels)]

    def span(level, part):
        if part == 0:
            return 0, R
        start = R if part == 1 else width_of(level, level + part - 1, levels)
        return start, width_of(level, level + part, levels) if part > 1 else width_of(level, level + 1, levels)

    def own(level, c0, c1):
        if level == 0:
            if c1 <= row_width:
                return row_ref.at[:, c0:c1]
            return t_ref.at[:, c0 - row_width : c1 - row_width]
        return own_ref.at[:, own_base[level] + c0 : own_base[level] + c1]

    def sib(level, c0, c1):
        return sib_ref.at[:, sib_base[level] + c0 : sib_base[level] + c1]

    def message(level, part):
        c0, c1 = span(level, part)
        index = first_message[level] + part
        return pltpu.make_async_remote_copy(
            src_ref=own(level, c0, c1),
            dst_ref=sib(level, c0, c1),
            send_sem=send_sem.at[index],
            recv_sem=recv_sem.at[index],
            device_id=partner[level],
            device_id_type=pl.DeviceIdType.MESH,
        )

    def side_slices(level):
        side = (position // 2**level) % 2
        mine = pl.ds(pl.multiple_of(side * R, R), R)
        other = pl.ds(pl.multiple_of((1 - side) * R, R), R)
        return mine, other

    def prepare(level):
        e = e_ref[level]
        eb_ref[...] = wide(jnp.concatenate([e[:R].T, e[R:].T], axis=1))
        et_ref[...] = tall(e)

    def begin(level):
        mine, other = side_slices(level)
        bd_ref[mine, other] = jnp.zeros((R, R), F32)
        bd_ref[other, mine] = jnp.zeros((R, R), F32)
        bd_ref[mine, mine] = own(level, 0, R)[...]
        message(level, 0).wait_recv()
        bd_ref[other, other] = sib(level, 0, R)[...]
        x = dot(eb_ref[...], tall(bd_ref[...]))
        h = dot(wide(x), et_ref[...])
        h = 0.5 * (h + h.T)
        a_ref[...] = h[:R, :R] + identity(R)
        h_ref[:R, :] = h[:R, R:]
        h_ref[R:, :] = h[R:, R:]

    def half(level):
        mine, other = side_slices(level)
        inverse = j_ref[...]
        inv_ref[...] = inverse
        stacked = wide(inverse)
        upper = dot(stacked, tall(h_ref[:R, :]))
        ut = upper.T
        u_ref[...] = upper
        left = wide(ut)
        a_ref[...] = h_ref[R:, :] + identity(R) - dot(left, tall(upper))
        message(level, 1).wait_recv()
        w = (levels - level) * R
        f_ref[mine, :w] = own(level, R, R + w)[...]
        f_ref[other, :w] = sib(level, R, R + w)[...]
        zb = z_base[level]
        for c0, c1 in chunks(0, w):
            forcing = dot(eb_ref[...], tall(f_ref[:, c0:c1]))
            z1 = dot(stacked, tall(forcing[:R]))
            f_ref[:R, c0:c1] = z1
            f_ref[R:, c0:c1] = forcing[R:] - dot(left, tall(z1))

    def finish(level):
        w = (levels - level) * R
        zb = z_base[level]
        stacked = wide(j_ref[...])
        for c0, c1 in chunks(0, w):
            f_ref[R:, c0:c1] = dot(stacked, tall(f_ref[R:, c0:c1]))
            value = f_ref[:, c0:c1]
            zt_ref[:, zb + c0 : zb + c1] = tall(value)
            zl_ref[zb + c0 : zb + c1, :] = wide(value.T)

    def update(level, row):
        part = row - level + 1
        message(level, part).wait_recv()
        c0, c1 = span(level, part)
        n0 = width_of(level + 1, row, levels)
        zb = z_base[level]
        shift = (row - level - 1) * R
        left = zl_ref[zb + shift : zb + shift + R, :]
        for d0, d1 in chunks(0, c1 - c0):
            value = own(level, c0 + d0, c0 + d1)[...] + sib(level, c0 + d0, c0 + d1)[...]
            value = value - dot(left, zt_ref[:, zb + shift + d0 : zb + shift + d1])
            own(level + 1, n0 + d0, n0 + d1)[...] = value
        if row == level + 1:
            message(level + 1, 0).start()
            message(level + 1, 1).start()
        else:
            message(level + 1, row - level).start()

    def gains(level):
        mine, _ = side_slices(level)
        e_own = e_ref[level, mine, :]
        w1 = dot3(e_own[:, :R], inv_ref[...].T)
        w2 = dot3(e_own[:, R:] - dot3(w1, u_ref[...]), j_ref[...].T)
        w = wide(jnp.concatenate([w1, w2], axis=1))
        zb = z_base[level]
        for c0, c1 in chunks(0, (levels - level) * R):
            g_ref[:, zb + c0 : zb + c1] = dot(w, zt_ref[:, zb + c0 : zb + c1])

    barrier = pltpu.get_barrier_semaphore()
    for device in partner:
        pl.semaphore_signal(barrier, inc=1, device_id=device, device_id_type=pl.DeviceIdType.MESH)
    pl.semaphore_wait(barrier, levels)
    message(0, 0).start()
    message(0, 1).start()
    prepare(0)
    fetch.wait()
    for b in range(y_ref.shape[0] // R):
        high, low = split(y_ref[blk(b), :])
        yh_ref[blk(b), :] = high
        yl_ref[blk(b), :] = low
    for k in range(1, levels):
        project(k, width_of(0, k, levels) - row_width, y_ref, yh_ref, yl_ref, t_ref)
    begin(0)

    starts = {(0, 0): [2], (0, 1): [3], (1, 0): [4], (1, 1): [5, 6, 7]}
    ahead = {(1, 0): [(0, 2)], (3, 0): [(2, 4)]}
    after = {
        (2, 0): [(0, 4)],
        (2, 1): [(1, 3), (0, 5), (0, 6)],
        (3, 0): [(1, 5), (1, 6)],
        (4, 0): [(3, 5), (3, 6)],
        (5, 0): [(4, 6)],
    }
    then = {(1, 1): [(0, 3)], (2, 1): [(1, 4)], (3, 1): [(2, 5), (2, 6)]}

    def step(i, carry):
        factor(a_ref, j_ref)
        for level in range(levels):

            @pl.when(i == 2 * level)
            def _(level=level):
                for part in starts.get((level, 0), []):
                    message(0, part).start()
                for pair in ahead.get((level, 0), []):
                    update(*pair)
                half(level)
                for pair in after.get((level, 0), []):
                    update(*pair)

            @pl.when(i == 2 * level + 1)
            def _(level=level):
                for part in starts.get((level, 1), []):
                    message(0, part).start()
                finish(level)
                for pair in after.get((level, 1), []):
                    update(*pair)
                if level < levels - 1:
                    update(level, level + 1)
                    for pair in then.get((level, 1), []):
                        update(*pair)
                    prepare(level + 1)
                gains(level)
                if level < levels - 1:
                    begin(level + 1)

        return carry

    lax.fori_loop(0, 2 * levels, step, 0)
    for level in range(levels):
        for part in range(levels + 1 - level):
            message(level, part).wait_send()


def final_kernel(y_hbm, u_hbm, li_hbm, g_ref, out_ref, y_ref, u_ref, li_ref, v_ref, x_ref, sems):
    fetches = [
        pltpu.make_async_copy(source, target, sems.at[i])
        for i, (source, target) in enumerate([(y_hbm, y_ref), (li_hbm, li_ref), (u_hbm, u_ref)])
    ]
    for fetch in fetches:
        fetch.start()
    levels = y_ref.shape[1] // R - 1
    slots = y_ref.shape[0]
    nb = slots // R
    for k in reversed(range(levels)):
        base = sum((levels - j) * R for j in range(k))
        inner = (levels - 1 - k) * R
        value = -g_ref[:, base + inner : base + inner + R]
        if inner > 0:
            value = value - dot3(g_ref[:, base : base + inner], v_ref[(k + 1) * R :, :])
        v_ref[blk(k), :] = value
    vt = tall(v_ref[...])
    fetches[0].wait()
    for b in range(nb):
        x_ref[blk(b), :] = y_ref[blk(b), levels * R :] + dot(wide(y_ref[blk(b), : levels * R]), vt)
    fetches[1].wait()
    fetches[2].wait()
    for b in reversed(range(nb)):
        value = dot3(li_ref[blk(b), :].T, x_ref[blk(b), :])
        out_ref[blk(b), :] = value
        if b > 0:
            x_ref[: b * R, :] = x_ref[: b * R, :] - dot3(u_ref[: b * R, blk(b)], value)


def f32(*shape):
    return jax.ShapeDtypeStruct(shape, F32)


def call(kernel, outs, ins, scratch=(), params=PARAMS, **kw):
    return pl.pallas_call(
        kernel,
        out_shape=outs,
        in_specs=ins,
        out_specs=jax.tree.map(lambda _: VMEM, outs),
        scratch_shapes=list(scratch),
        compiler_params=params,
        **kw,
    )


def shards(points, order, counts, basis, right_side, coupling):
    slots = points.shape[1]
    levels = basis.shape[1] // R
    columns = levels * R + right_side.shape[1]
    packed = width_of(0, levels, levels)
    t, y, u, li = call(
        leaf_kernel,
        (f32(R, columns), f32(slots, columns), f32(slots, slots), f32(slots, R)),
        [SMEM, VMEM, VMEM, VMEM, VMEM],
        [
            pltpu.VMEM((R, R), F32),
            pltpu.VMEM((R, R), F32),
            pltpu.VMEM((3 * R, slots + columns), BF16),
            pltpu.VMEM((slots, 3 * R), BF16),
            pltpu.VMEM((slots, columns), BF16),
            pltpu.VMEM((slots, columns), BF16),
            pltpu.VMEM((8, slots), F32),
            pltpu.VMEM((slots, 8), F32),
        ],
    )(counts, points, order, basis, right_side)
    own_width = sum(width_of(k, levels, levels) for k in range(1, levels))
    gain_width = sum((levels - k) * R for k in range(levels))
    messages = sum(levels + 1 - k for k in range(levels))
    g = call(
        functools.partial(levels_kernel, levels),
        f32(R, gain_width),
        [VMEM, ANY, VMEM],
        [
            pltpu.VMEM((R, packed - columns), F32),
            pltpu.VMEM((slots, columns), F32),
            pltpu.VMEM((slots, columns), BF16),
            pltpu.VMEM((slots, columns), BF16),
            pltpu.VMEM((R, own_width), F32),
            pltpu.VMEM((R, own_width + packed), F32),
            pltpu.VMEM((6 * R, gain_width), BF16),
            pltpu.VMEM((gain_width, 6 * R), BF16),
            pltpu.VMEM((2 * R, 2 * R), F32),
            pltpu.VMEM((2 * R, R), F32),
            pltpu.VMEM((2 * R, levels * R), F32),
            pltpu.VMEM((2 * R, 6 * R), BF16),
            pltpu.VMEM((6 * R, 2 * R), BF16),
            pltpu.VMEM((R, R), F32),
            pltpu.VMEM((R, R), F32),
            pltpu.VMEM((R, R), F32),
            pltpu.VMEM((R, R), F32),
            pltpu.SemaphoreType.DMA((messages,)),
            pltpu.SemaphoreType.DMA((messages,)),
            pltpu.SemaphoreType.DMA,
        ],
        pltpu.CompilerParams(
            vmem_limit_bytes=56 * 1024 * 1024, collective_id=0, has_side_effects=True
        ),
    )(t, y, coupling)
    return call(
        final_kernel,
        f32(slots, columns - levels * R),
        [ANY] * 3 + [VMEM],
        [
            pltpu.VMEM((slots, columns), F32),
            pltpu.VMEM((slots, slots), F32),
            pltpu.VMEM((slots, R), F32),
            pltpu.VMEM((levels * R, R), F32),
            pltpu.VMEM((slots, R), F32),
            pltpu.SemaphoreType.DMA((3,)),
        ],
    )(y, u, li, g)


def solution(mesh):
    placed = (
        P(None, ("leaf", "sub")),
        P(("leaf", "sub"), None),
        P(("leaf", "sub")),
        P(("leaf", "sub"), None),
        P(("leaf", "sub"), None),
        P(),
    )
    return jax.shard_map(
        shards, mesh=mesh, in_specs=placed, out_specs=P(("leaf", "sub"), None), check_vma=False
    )
```

```python
import functools

import jax
import jax.numpy as jnp
from jax import lax
from jax.experimental import pallas as pl
from jax.experimental.pallas import tpu as pltpu
from jax.sharding import PartitionSpec as P

R = 128
GAMMA_RATE = 2.0
NUGGET_VALUE = 1.0
F32 = jnp.float32
BF16 = jnp.bfloat16
VMEM = pl.BlockSpec(memory_space=pltpu.VMEM)
SMEM = pl.BlockSpec(memory_space=pltpu.SMEM)
ANY = pl.BlockSpec(memory_space=pl.ANY)
PARAMS = pltpu.CompilerParams(vmem_limit_bytes=56 * 1024 * 1024)


def split(x):
    high = x.astype(BF16)
    low = (x - high.astype(F32)).astype(BF16)
    return high, low


def dot(a, b):
    return jnp.dot(a, b, preferred_element_type=F32)


def wide(x):
    high, low = split(x)
    return jnp.concatenate([high, high, low], axis=1)


def tall(x):
    high, low = split(x)
    return jnp.concatenate([high, low, high], axis=0)


def dot3(a, b):
    return dot(wide(a), tall(b))


def identity(n):
    rows = lax.broadcasted_iota(jnp.int32, (n, n), 0)
    cols = lax.broadcasted_iota(jnp.int32, (n, n), 1)
    return (rows == cols).astype(F32)


def factor(a_ref, j_ref):
    n = R
    groups = n // 8
    sub = lax.broadcasted_iota(jnp.int32, (8, n), 0)
    lane = lax.broadcasted_iota(jnp.int32, (8, n), 1)
    rows = [a_ref[8 * g : 8 * g + 8, :] for g in range(groups)]

    def column(x, c):
        return jnp.take_along_axis(x, jnp.full((8, n), c, jnp.int32), axis=1, mode="promise_in_bounds")

    def row(x, r):
        return jnp.broadcast_to(x[r : r + 1, :], (8, n))

    for p in range(groups):
        r0 = 8 * p
        inside = (lane >= r0) & (lane < r0 + 8)
        cols = [column(rows[p], r0 + c) for c in range(8)]
        a = [[row(cols[c], s) for c in range(s + 1)] for s in range(8)]
        panel = jnp.where(inside, (sub == lane - r0).astype(F32), rows[p])
        rs = [None] * 8
        low = [[None] * 8 for _ in range(8)]
        up = [row(panel, r) for r in range(8)]
        later = range(p + 1, groups)
        m = {g: [column(rows[g], r0 + r) for r in range(8)] for g in later}
        acc = {g: jnp.where(inside, 0.0, rows[g]) for g in later}
        for r in range(8):
            rs[r] = lax.rsqrt(a[r][r])
            for s in range(r + 1, 8):
                low[s][r] = a[s][r] * rs[r]
            for s in range(r + 1, 8):
                for c in range(r + 1, s + 1):
                    a[s][c] = a[s][c] - low[s][r] * low[c][r]
            up[r] = up[r] * rs[r]
            for s in range(r + 1, 8):
                up[s] = up[s] - low[s][r] * up[r]
            for g in later:
                m[g][r] = m[g][r] * rs[r]
                for s in range(r + 1, 8):
                    m[g][s] = m[g][s] - low[s][r] * m[g][r]
                acc[g] = acc[g] - m[g][r] * up[r]
        for g in later:
            rows[g] = acc[g]
        done = up[0]
        for r in range(1, 8):
            done = jnp.where(sub == r, up[r], done)
        j_ref[r0 : r0 + 8, :] = jnp.where(lane < r0 + 8, done, 0.0)


def chunks(start, stop, size=256):
    return [(c, min(c + size, stop)) for c in range(start, stop, size)]


def blk(i):
    return slice(i * R, (i + 1) * R)


def leaf_kernel(
    count_ref, points_ref, order_ref, basis_hbm, rhs_hbm,
    t_ref, y_hbm, u_hbm, li_hbm, basis_ref, rhs_ref, y_ref, u_ref, li_ref,
    a_ref, j_ref, right_ref, left_ref, yh_ref, yl_ref, xr_ref, xc_ref, in_sems, out_sems,
):
    fetches = [
        pltpu.make_async_copy(basis_hbm, basis_ref, in_sems.at[0]),
        pltpu.make_async_copy(rhs_hbm, rhs_ref, in_sems.at[1]),
    ]
    for fetch in fetches:
        fetch.start()

    def stores(b):
        return [
            pltpu.make_async_copy(y_ref.at[blk(b), :], y_hbm.at[blk(b), :], out_sems.at[3 * b]),
            pltpu.make_async_copy(li_ref.at[blk(b), :], li_hbm.at[blk(b), :], out_sems.at[3 * b + 1]),
            pltpu.make_async_copy(u_ref.at[blk(b), b * R :], u_hbm.at[blk(b), b * R :], out_sems.at[3 * b + 2]),
        ]

    slots, columns = y_ref.shape
    nb = slots // R
    levels = basis_ref.shape[1] // R
    count = count_ref[0]
    points = points_ref[...]
    high = points.astype(BF16)
    middle = (points - high.astype(F32)).astype(BF16)
    low = (points - high.astype(F32) - middle.astype(F32)).astype(BF16)
    xr_ref[...] = jnp.zeros_like(xr_ref)
    source = lax.broadcasted_iota(jnp.int32, (slots, 256), 0)
    for c0, c1 in chunks(0, slots, 256):
        chosen = (source == order_ref[:, c0:c1]).astype(F32).astype(BF16)
        xr_ref[:3, c0:c1] = dot(high, chosen) + dot(middle, chosen) + dot(low, chosen)
    for b in range(nb):
        xc_ref[blk(b), :] = xr_ref[:, blk(b)].T
    live_lane = (lax.broadcasted_iota(jnp.int32, (1, slots), 1) < count).astype(F32)
    live_sub = (lax.broadcasted_iota(jnp.int32, (slots, 1), 0) < count).astype(F32)
    for b in range(nb):
        live_b = live_sub[blk(b), :]
        for c0, c1 in chunks(b * R, slots, 128):
            dist = None
            for d in range(3):
                diff = xc_ref[blk(b), d : d + 1] - xr_ref[d : d + 1, c0:c1]
                dist = diff * diff if dist is None else dist + diff * diff
            kern = jnp.exp(-GAMMA_RATE * dist) * live_b * live_lane[:, c0:c1]
            if c0 == b * R:
                kern = kern + NUGGET_VALUE * identity(R)
            u_ref[blk(b), c0:c1] = kern

    for fetch in fetches:
        fetch.wait()
    for b in range(nb):
        live_b = live_sub[blk(b), :]
        y_ref[blk(b), : levels * R] = basis_ref[blk(b), :] * live_b
        y_ref[blk(b), levels * R :] = rhs_ref[blk(b), :] * live_b

    def step(b, carry):
        here = pl.ds(pl.multiple_of(b * R, R), R)
        a_ref[...] = u_ref[here, here]
        factor(a_ref, j_ref)
        li_ref[here, :] = j_ref[...]
        for static_b in range(nb):

            @pl.when(b == static_b)
            def _(b=static_b):
                inv = wide(j_ref[...])
                for c0, c1 in chunks((b + 1) * R, slots, 256):
                    new = dot(inv, tall(u_ref[blk(b), c0:c1]))
                    u_ref[blk(b), c0:c1] = new
                    right_ref[:, c0:c1] = tall(new)
                    for e0, e1 in chunks(c0, c1, R):
                        left_ref[e0:e1, :] = wide(new[:, e0 - c0 : e1 - c0].T)
                for c0, c1 in chunks(0, columns, 256):
                    new = dot(inv, tall(y_ref[blk(b), c0:c1]))
                    y_ref[blk(b), c0:c1] = new
                    stacked = tall(new)
                    right_ref[:, slots + c0 : slots + c1] = stacked
                    yh_ref[blk(b), c0:c1] = stacked[:R]
                    yl_ref[blk(b), c0:c1] = stacked[R : 2 * R]
                for i in range(b + 1, nb):
                    left = left_ref[blk(i), :]
                    for c0, c1 in chunks(i * R, slots, 256):
                        u_ref[blk(i), c0:c1] = u_ref[blk(i), c0:c1] - dot(left, right_ref[:, c0:c1])
                    for c0, c1 in chunks(0, columns, 256):
                        y_ref[blk(i), c0:c1] = y_ref[blk(i), c0:c1] - dot(
                            left, right_ref[:, slots + c0 : slots + c1]
                        )
                for store in stores(b):
                    store.start()

        return carry

    lax.fori_loop(0, nb, step, 0)
    project(0, 0, y_ref, yh_ref, yl_ref, t_ref)
    for b in range(nb):
        for store in stores(b):
            store.wait()


def project(k, offset, y_ref, yh_ref, yl_ref, t_ref):
    columns = y_ref.shape[1]
    high, low = split(y_ref[:, blk(k)].T)
    for c0, c1 in chunks(k * R, columns, 256):
        yh = yh_ref[:, c0:c1]
        value = dot(high, yh) + dot(high, yl_ref[:, c0:c1]) + dot(low, yh)
        t_ref[:, offset + c0 - k * R : offset + c1 - k * R] = value


def width_of(level, row, levels):
    return sum((levels + 1 - k) * R for k in range(level, row))


def levels_kernel(
    levels, row_ref, y_hbm, e_hbm, g_ref,
    e_ref, t_ref, y_ref, yh_ref, yl_ref, own_ref, sib_ref, zt_ref, zl_ref, bd_ref, h_ref, f_ref, eb_ref, et_ref, u_ref, inv_ref, a_ref, j_ref,
    send_sem, recv_sem, y_sem, e_sem,
):
    fetch_e = pltpu.make_async_copy(e_hbm, e_ref, e_sem)
    fetch_e.start()
    fetch = pltpu.make_async_copy(y_hbm, y_ref, y_sem)
    fetch.start()
    row_width = row_ref.shape[1]
    leaf, sub = lax.axis_index("leaf"), lax.axis_index("sub")
    core, z, y = leaf % 2, (leaf // 2) % 4, leaf // 8
    partner = [
        (leaf, sub + 1 - 2 * (sub % 2)),
        (leaf, 3 - sub),
        (leaf + 1 - 2 * core, sub),
        (y * 8 + (z + 1 - 2 * (z % 2)) * 2 + core, sub),
        (y * 8 + (3 - z) * 2 + core, sub),
        ((y + 1 - 2 * (y % 2)) * 8 + z * 2 + core, sub),
        ((3 - y) * 8 + z * 2 + core, sub),
    ]
    position = leaf * 4 + sub
    total = [width_of(k, levels, levels) for k in range(levels)]
    own_base = [0] + [sum(total[1:k]) for k in range(1, levels)]
    sib_base = [sum(total[:k]) for k in range(levels)]
    z_base = [sum((levels - j) * R for j in range(k)) for k in range(levels)]
    first_message = [sum(levels + 1 - j for j in range(k)) for k in range(levels)]

    def span(level, part):
        if part == 0:
            return 0, R
        start = R if part == 1 else width_of(level, level + part - 1, levels)
        return start, width_of(level, level + part, levels) if part > 1 else width_of(level, level + 1, levels)

    def own(level, c0, c1):
        if level == 0:
            if c1 <= row_width:
                return row_ref.at[:, c0:c1]
            return t_ref.at[:, c0 - row_width : c1 - row_width]
        return own_ref.at[:, own_base[level] + c0 : own_base[level] + c1]

    def sib(level, c0, c1):
        return sib_ref.at[:, sib_base[level] + c0 : sib_base[level] + c1]

    def message(level, part):
        c0, c1 = span(level, part)
        index = first_message[level] + part
        return pltpu.make_async_remote_copy(
            src_ref=own(level, c0, c1),
            dst_ref=sib(level, c0, c1),
            send_sem=send_sem.at[index],
            recv_sem=recv_sem.at[index],
            device_id=partner[level],
            device_id_type=pl.DeviceIdType.MESH,
        )

    def side_slices(level):
        side = (position // 2**level) % 2
        mine = pl.ds(pl.multiple_of(side * R, R), R)
        other = pl.ds(pl.multiple_of((1 - side) * R, R), R)
        return mine, other

    def prepare(level):
        e = e_ref[level]
        eb_ref[...] = wide(jnp.concatenate([e[:R].T, e[R:].T], axis=1))
        et_ref[...] = tall(e)

    def begin(level):
        mine, other = side_slices(level)
        bd_ref[mine, other] = jnp.zeros((R, R), F32)
        bd_ref[other, mine] = jnp.zeros((R, R), F32)
        bd_ref[mine, mine] = own(level, 0, R)[...]
        message(level, 0).wait_recv()
        bd_ref[other, other] = sib(level, 0, R)[...]
        x = dot(eb_ref[...], tall(bd_ref[...]))
        h = dot(wide(x), et_ref[...])
        h = 0.5 * (h + h.T)
        a_ref[...] = h[:R, :R] + identity(R)
        h_ref[:R, :] = h[:R, R:]
        h_ref[R:, :] = h[R:, R:]

    def half(level):
        mine, other = side_slices(level)
        inverse = j_ref[...]
        inv_ref[...] = inverse
        stacked = wide(inverse)
        upper = dot(stacked, tall(h_ref[:R, :]))
        ut = upper.T
        u_ref[...] = upper
        left = wide(ut)
        a_ref[...] = h_ref[R:, :] + identity(R) - dot(left, tall(upper))
        message(level, 1).wait_recv()
        w = (levels - level) * R
        f_ref[mine, :w] = own(level, R, R + w)[...]
        f_ref[other, :w] = sib(level, R, R + w)[...]
        zb = z_base[level]
        for c0, c1 in chunks(0, w):
            forcing = dot(eb_ref[...], tall(f_ref[:, c0:c1]))
            z1 = dot(stacked, tall(forcing[:R]))
            f_ref[:R, c0:c1] = z1
            f_ref[R:, c0:c1] = forcing[R:] - dot(left, tall(z1))

    def finish(level):
        w = (levels - level) * R
        zb = z_base[level]
        stacked = wide(j_ref[...])
        for c0, c1 in chunks(0, w):
            f_ref[R:, c0:c1] = dot(stacked, tall(f_ref[R:, c0:c1]))
            value = f_ref[:, c0:c1]
            zt_ref[:, zb + c0 : zb + c1] = tall(value)
            zl_ref[zb + c0 : zb + c1, :] = wide(value.T)

    def update(level, row):
        part = row - level + 1
        message(level, part).wait_recv()
        c0, c1 = span(level, part)
        n0 = width_of(level + 1, row, levels)
        zb = z_base[level]
        shift = (row - level - 1) * R
        left = zl_ref[zb + shift : zb + shift + R, :]
        for d0, d1 in chunks(0, c1 - c0):
            value = own(level, c0 + d0, c0 + d1)[...] + sib(level, c0 + d0, c0 + d1)[...]
            value = value - dot(left, zt_ref[:, zb + shift + d0 : zb + shift + d1])
            own(level + 1, n0 + d0, n0 + d1)[...] = value
        if row == level + 1:
            message(level + 1, 0).start()
            message(level + 1, 1).start()
        else:
            message(level + 1, row - level).start()

    def gains(level):
        mine, _ = side_slices(level)
        e_own = e_ref[level, mine, :]
        w1 = dot3(e_own[:, :R], inv_ref[...].T)
        w2 = dot3(e_own[:, R:] - dot3(w1, u_ref[...]), j_ref[...].T)
        w = wide(jnp.concatenate([w1, w2], axis=1))
        zb = z_base[level]
        for c0, c1 in chunks(0, (levels - level) * R):
            g_ref[:, zb + c0 : zb + c1] = dot(w, zt_ref[:, zb + c0 : zb + c1])

    barrier = pltpu.get_barrier_semaphore()
    for device in partner:
        pl.semaphore_signal(barrier, inc=1, device_id=device, device_id_type=pl.DeviceIdType.MESH)
    pl.semaphore_wait(barrier, levels)
    message(0, 0).start()
    message(0, 1).start()
    fetch_e.wait()
    prepare(0)
    fetch.wait()
    for b in range(y_ref.shape[0] // R):
        high, low = split(y_ref[blk(b), :])
        yh_ref[blk(b), :] = high
        yl_ref[blk(b), :] = low
    for k in range(1, levels):
        project(k, width_of(0, k, levels) - row_width, y_ref, yh_ref, yl_ref, t_ref)
    begin(0)

    starts = {(0, 0): [2], (0, 1): [3], (1, 0): [4], (1, 1): [5, 6, 7]}
    ahead = {(1, 0): [(0, 2)], (3, 0): [(2, 4)]}
    after = {
        (2, 0): [(0, 4)],
        (2, 1): [(1, 3), (0, 5), (0, 6)],
        (3, 0): [(1, 5), (1, 6)],
        (4, 0): [(3, 5), (3, 6)],
        (5, 0): [(4, 6)],
    }
    then = {(1, 1): [(0, 3)], (2, 1): [(1, 4)], (3, 1): [(2, 5), (2, 6)]}

    def step(i, carry):
        factor(a_ref, j_ref)
        for level in range(levels):

            @pl.when(i == 2 * level)
            def _(level=level):
                for part in starts.get((level, 0), []):
                    message(0, part).start()
                for pair in ahead.get((level, 0), []):
                    update(*pair)
                half(level)
                for pair in after.get((level, 0), []):
                    update(*pair)

            @pl.when(i == 2 * level + 1)
            def _(level=level):
                for part in starts.get((level, 1), []):
                    message(0, part).start()
                finish(level)
                for pair in after.get((level, 1), []):
                    update(*pair)
                if level < levels - 1:
                    update(level, level + 1)
                    for pair in then.get((level, 1), []):
                        update(*pair)
                    prepare(level + 1)
                gains(level)
                if level < levels - 1:
                    begin(level + 1)

        return carry

    lax.fori_loop(0, 2 * levels, step, 0)
    for level in range(levels):
        for part in range(levels + 1 - level):
            message(level, part).wait_send()


def final_kernel(y_hbm, u_hbm, li_hbm, g_ref, out_ref, y_ref, u_ref, li_ref, v_ref, x_ref, sems):
    fetches = [
        pltpu.make_async_copy(source, target, sems.at[i])
        for i, (source, target) in enumerate([(y_hbm, y_ref), (li_hbm, li_ref), (u_hbm, u_ref)])
    ]
    for fetch in fetches:
        fetch.start()
    levels = y_ref.shape[1] // R - 1
    slots = y_ref.shape[0]
    nb = slots // R
    for k in reversed(range(levels)):
        base = sum((levels - j) * R for j in range(k))
        inner = (levels - 1 - k) * R
        value = -g_ref[:, base + inner : base + inner + R]
        if inner > 0:
            value = value - dot3(g_ref[:, base : base + inner], v_ref[(k + 1) * R :, :])
        v_ref[blk(k), :] = value
    vt = tall(v_ref[...])
    fetches[0].wait()
    for b in range(nb):
        x_ref[blk(b), :] = y_ref[blk(b), levels * R :] + dot(wide(y_ref[blk(b), : levels * R]), vt)
    fetches[1].wait()
    fetches[2].wait()
    for b in reversed(range(nb)):
        value = dot3(li_ref[blk(b), :].T, x_ref[blk(b), :])
        out_ref[blk(b), :] = value
        if b > 0:
            x_ref[: b * R, :] = x_ref[: b * R, :] - dot3(u_ref[: b * R, blk(b)], value)


def f32(*shape):
    return jax.ShapeDtypeStruct(shape, F32)


def call(kernel, outs, ins, scratch=(), params=PARAMS, places=None, **kw):
    return pl.pallas_call(
        kernel,
        out_shape=outs,
        in_specs=ins,
        out_specs=places or jax.tree.map(lambda _: VMEM, outs),
        scratch_shapes=list(scratch),
        compiler_params=params,
        **kw,
    )


def shards(points, order, counts, basis, right_side, coupling):
    slots = points.shape[1]
    levels = basis.shape[1] // R
    columns = levels * R + right_side.shape[1]
    packed = width_of(0, levels, levels)
    t, y, u, li = call(
        leaf_kernel,
        (f32(R, columns), f32(slots, columns), f32(slots, slots), f32(slots, R)),
        [SMEM, VMEM, VMEM, ANY, ANY],
        [
            pltpu.VMEM(basis.shape, F32),
            pltpu.VMEM(right_side.shape, F32),
            pltpu.VMEM((slots, columns), F32),
            pltpu.VMEM((slots, slots), F32),
            pltpu.VMEM((slots, R), F32),
            pltpu.VMEM((R, R), F32),
            pltpu.VMEM((R, R), F32),
            pltpu.VMEM((3 * R, slots + columns), BF16),
            pltpu.VMEM((slots, 3 * R), BF16),
            pltpu.VMEM((slots, columns), BF16),
            pltpu.VMEM((slots, columns), BF16),
            pltpu.VMEM((8, slots), F32),
            pltpu.VMEM((slots, 8), F32),
            pltpu.SemaphoreType.DMA((2,)),
            pltpu.SemaphoreType.DMA((3 * slots // R,)),
        ],
        places=(VMEM, ANY, ANY, ANY),
    )(counts, points, order, basis, right_side)
    own_width = sum(width_of(k, levels, levels) for k in range(1, levels))
    gain_width = sum((levels - k) * R for k in range(levels))
    messages = sum(levels + 1 - k for k in range(levels))
    g = call(
        functools.partial(levels_kernel, levels),
        f32(R, gain_width),
        [VMEM, ANY, ANY],
        [
            pltpu.VMEM(coupling.shape, F32),
            pltpu.VMEM((R, packed - columns), F32),
            pltpu.VMEM((slots, columns), F32),
            pltpu.VMEM((slots, columns), BF16),
            pltpu.VMEM((slots, columns), BF16),
            pltpu.VMEM((R, own_width), F32),
            pltpu.VMEM((R, own_width + packed), F32),
            pltpu.VMEM((6 * R, gain_width), BF16),
            pltpu.VMEM((gain_width, 6 * R), BF16),
            pltpu.VMEM((2 * R, 2 * R), F32),
            pltpu.VMEM((2 * R, R), F32),
            pltpu.VMEM((2 * R, levels * R), F32),
            pltpu.VMEM((2 * R, 6 * R), BF16),
            pltpu.VMEM((6 * R, 2 * R), BF16),
            pltpu.VMEM((R, R), F32),
            pltpu.VMEM((R, R), F32),
            pltpu.VMEM((R, R), F32),
            pltpu.VMEM((R, R), F32),
            pltpu.SemaphoreType.DMA((messages,)),
            pltpu.SemaphoreType.DMA((messages,)),
            pltpu.SemaphoreType.DMA,
            pltpu.SemaphoreType.DMA,
        ],
        pltpu.CompilerParams(
            vmem_limit_bytes=56 * 1024 * 1024, collective_id=0, has_side_effects=True
        ),
    )(t, y, coupling)
    return call(
        final_kernel,
        f32(slots, columns - levels * R),
        [ANY] * 3 + [VMEM],
        [
            pltpu.VMEM((slots, columns), F32),
            pltpu.VMEM((slots, slots), F32),
            pltpu.VMEM((slots, R), F32),
            pltpu.VMEM((levels * R, R), F32),
            pltpu.VMEM((slots, R), F32),
            pltpu.SemaphoreType.DMA((3,)),
        ],
    )(y, u, li, g)


def solution(mesh):
    placed = (
        P(None, ("leaf", "sub")),
        P(("leaf", "sub"), None),
        P(("leaf", "sub")),
        P(("leaf", "sub"), None),
        P(("leaf", "sub"), None),
        P(),
    )
    return jax.shard_map(
        shards, mesh=mesh, in_specs=placed, out_specs=P(("leaf", "sub"), None), check_vma=False
    )
```
